32 devices in a mesh: dp: 8 (over y, x, core), tensor: 4 (over z).
Axes of the slice: x: 2, y: 2, z: 4, core: 2. Of those that a mesh axis runs over, the one named last changes fastest.
Arguments:
- tokens: bfloat16 [16, 512, 2048], P('dp', 'tensor'), may hold values from -6 to 6
- lengths: int32 [16], P('dp'), may hold values from 128 to 512, as said below
- norm_gain: bfloat16 [2048], P('dp'), may hold values from 0.5 to 1.5
- mixer_in: bfloat16 [2048, 3, 2048], P('dp', None, 'tensor'), may hold values from -0.125 to 0.125
- lower_bound: bfloat16 [2048], P(('tensor', 'dp')), may hold values from 0.049804688 to 0.98828125
- head_gain: bfloat16 [128], P('dp'), may hold values from 0.5 to 1.5
- head_merge: bfloat16 [2048, 2048], P(('tensor', 'dp')), may hold values from -0.125 to 0.125
- feed_gain: bfloat16 [2048], P('dp'), may hold values from 0.5 to 1.5
- gate_up: bfloat16 [2048, 2, 5632], P('dp', None, 'tensor'), may hold values from -0.125 to 0.125
- down_weight: bfloat16 [5632, 2048], P(('tensor', 'dp')), may hold values from -0.078125 to 0.078125
- out_grad: bfloat16 [16, 512, 2048], P('dp', 'tensor'), may hold values from -6 to 6
Outputs:
- block_out: bfloat16 [16, 512, 2048], P('dp', 'tensor')
- input_grad: bfloat16 [16, 512, 2048], P('dp', 'tensor')
- norm_grad: float32 [2048], P('dp')
- mixer_grad: float32 [2048, 3, 2048], P('dp', None, 'tensor')
- bound_grad: float32 [2048], P(('tensor', 'dp'))
- head_grad: float32 [128], P('dp')
- merge_grad: float32 [2048, 2048], P(('tensor', 'dp'))
- feed_grad: float32 [2048], P('dp')
- gates_grad: float32 [2048, 2, 5632], P('dp', None, 'tensor')
- down_grad: float32 [5632, 2048], P(('tensor', 'dp'))
The draws below stay inside these ranges and needn't reach their ends.
Inputs may be any that keep to these rules, and one draw needn't show every extreme that they name: Slots 0 to lengths[s] - 1 of sequence s are valid; some sequence has exactly 512 valid slots and some other exactly 128.
All inputs are finite; a program needn't handle non-finite values.
Results may differ from the reference program's by a relative error of at most 0.024.
Values may be sent and summed in bfloat16 or wider, within the bound.
No kernel may reach another device: no remote copies, remote signals or barrier semaphores. Data moves between devices by JAX's collectives and lax.ppermute only.
A program may use at most 256 MiB of HBM per device.

```python
import jax
import jax.numpy as jnp
from jax import lax

D = 2048
FF = 5632
HEAD_DIM = 128
L = 512
GROUP = 32
SEQS = 16


def draw_lengths(key, part):
    first_key, second_key, third_key = jax.random.split(key, 3)
    drawn_len = jax.random.randint(first_key, (SEQS,), L // 4, L + 1)
    longest = jax.random.randint(second_key, (), 0, SEQS)
    shortest = (longest + jax.random.randint(third_key, (), 1, SEQS)) % SEQS
    slot_ids = jnp.arange(SEQS)
    drawn_len = jnp.where(slot_ids == longest, L, drawn_len)
    drawn_len = jnp.where(slot_ids == shortest, L // 4, drawn_len)
    return drawn_len.astype(jnp.int32)


def level_of(own_key, shape, shards, low, high):
    def one(axis_at, parts):
        steps = jax.random.uniform(jax.random.fold_in(jax.random.fold_in(own_key, 6), axis_at), (parts,), jnp.float32, low / len(shards), high / len(shards))
        return jnp.repeat(jnp.exp(steps), shape[axis_at] // parts).reshape((-1,) + (1,) * (len(shape) - axis_at - 1))

    level = one(*shards[0])
    for cut in shards[1:]:
        level = level * one(*cut)
    return level


def gaussian(own_key, extent, scale, limit, shards=(), kind=jnp.bfloat16):
    factor_of = level_of(own_key, extent, shards, -0.22, 0.18) if shards else 1.0
    drawn = jax.random.normal(own_key, extent, jnp.float32) * scale * factor_of
    return jnp.minimum(jnp.maximum(drawn, -limit), limit).astype(kind)


def setup_inputs(seed: int = 0) -> dict:
    seeds = jax.random.split(jax.random.key(seed), 12)
    tokens = gaussian(seeds[0], (SEQS, L, D), 1.0, 6.0, ((0, 8), (1, 4)))
    lengths = draw_lengths(jax.random.fold_in(seeds[11], 71), 0)
    norm_gain = jnp.clip(1.0 + 0.1 * jax.random.normal(seeds[2], (D,), jnp.float32), 0.5, 1.5).astype(jnp.bfloat16)
    mixer_in = gaussian(seeds[3], (D, 3, D), D ** -0.5, 0.125, ((0, 8), (2, 4)))
    lower_bound = jnp.clip(0.049804688 + 0.93847656 * jax.random.uniform(seeds[4], (D,), jnp.float32) ** level_of(seeds[4], (D,), ((0, 32),), -0.2, 0.2), 0.049804688, 0.98828125).astype(jnp.bfloat16)
    head_gain = jnp.clip(1.0 + 0.1 * jax.random.normal(seeds[5], (HEAD_DIM,), jnp.float32), 0.5, 1.5).astype(jnp.bfloat16)
    head_merge = gaussian(seeds[6], (D, D), D ** -0.5, 0.125, ((0, 32),))
    feed_gain = jnp.clip(1.0 + 0.1 * jax.random.normal(seeds[7], (D,), jnp.float32), 0.5, 1.5).astype(jnp.bfloat16)
    gate_up = gaussian(seeds[8], (D, 2, FF), D ** -0.5, 0.125, ((0, 8), (2, 4)))
    down_weight = gaussian(seeds[9], (FF, D), FF ** -0.5, 0.078125, ((0, 32),))
    out_grad = gaussian(seeds[10], (SEQS, L, D), 1.0, 6.0, ((0, 8), (1, 4)))
    return dict(tokens=tokens, lengths=lengths, norm_gain=norm_gain, mixer_in=mixer_in, lower_bound=lower_bound, head_gain=head_gain, head_merge=head_merge, feed_gain=feed_gain, gate_up=gate_up, down_weight=down_weight, out_grad=out_grad)


EPS = 1e-06
HIGH = lax.Precision.HIGHEST

@jax.custom_vjp
def low(v):
    return lax.optimization_barrier(v.astype(jnp.bfloat16)).astype(jnp.float32)

@jax.custom_vjp
def low_back(v):
    return v

def low_keep(v):
    return (low(v), None)

def low_pass(kept, grad):
    return (grad,)

def back_keep(v):
    return (v, None)

def back_low(kept, grad):
    return (low(grad),)
low.defvjp(low_keep, low_pass)
low_back.defvjp(back_keep, back_low)

def group_step(state, block):
    queries, keys_in, values_in, log_gate = block
    cumulative = jnp.cumsum(log_gate, axis=0)
    group_end = cumulative[-1]
    carried_in = jnp.einsum('the,hef->thf', queries * jnp.exp(cumulative), state, precision=HIGH)
    length = cumulative.shape[0]
    causal = jnp.arange(length)[:, None] >= jnp.arange(length)[None, :]
    causal_four = causal[:, :, None, None]
    spread = jnp.where(causal_four, cumulative[:, None] - cumulative[None, :], -60.0)
    decays = jnp.exp(spread) * causal_four.astype(jnp.float32)
    scores = lax.optimization_barrier(jnp.sum(queries[:, None] * keys_in[None, :] * decays, axis=-1))
    within = jnp.einsum('tsh,shf->thf', scores, values_in, precision=HIGH)
    carried = keys_in * jnp.exp(group_end[None] - cumulative)
    update = jnp.einsum('she,shf->hef', carried, values_in, precision=HIGH)
    new_state = jnp.exp(group_end)[:, :, None] * state + update
    return (new_state, carried_in + within)

def recurrence(queries, keys_in, values_in, log_gate):
    total_rows, head_count, head_width = queries.shape
    blocks = total_rows // GROUP
    stacked = tuple((member.reshape(blocks, GROUP, head_count, head_width) for member in (queries, keys_in, values_in, log_gate)))
    initial = jnp.zeros((head_count, head_width, head_width), jnp.float32)
    last_state, outputs = lax.scan(jax.checkpoint(group_step), initial, stacked)
    return outputs.reshape(total_rows, head_count, head_width)

def rms_rows(values, gain_vec):
    return values * lax.rsqrt(lax.optimization_barrier(jnp.mean(values * values, axis=-1, keepdims=True)) + EPS) * gain_vec

def matmul(first_mat, second_mat):
    return jnp.dot(first_mat, second_mat, precision=HIGH, preferred_element_type=jnp.float32)

def block_forward(tokens_row, valid_mask, norm_gain, mixer_in, lower_bound, head_gain, head_merge, feed_gain, gate_up, down_weight):
    seq_len, model_width = tokens_row.shape
    masked = tokens_row * valid_mask[:, None]
    first_in = low(rms_rows(masked, norm_gain))
    projected = low_back(matmul(first_in, mixer_in.reshape(model_width, 3 * model_width)))
    query_pre = projected[:, :model_width]
    forget_pre = projected[:, model_width:2 * model_width]
    value_pre = projected[:, 2 * model_width:]
    queries = low(jax.nn.silu(query_pre))
    forget = lower_bound + (1.0 - lower_bound) * jax.nn.sigmoid(forget_pre)
    keys_in = low(1.0 - forget)
    values_in = low(value_pre)
    log_gate = jnp.log(forget)
    head_width = head_gain.shape[0]
    head_shape = (seq_len, model_width // head_width, head_width)
    mixed_rows = recurrence(queries.reshape(head_shape), keys_in.reshape(head_shape), values_in.reshape(head_shape), log_gate.reshape(head_shape))
    scaling = lax.rsqrt(lax.optimization_barrier(jnp.mean(mixed_rows * mixed_rows, axis=-1, keepdims=True)) + EPS)
    head_out = low((mixed_rows * scaling * head_gain).reshape(seq_len, model_width))
    middle = masked + low_back(matmul(head_out, head_merge))
    second_in = low(rms_rows(middle, feed_gain))
    gate_cols = low_back(matmul(second_in, gate_up.reshape(model_width, -1)))
    hidden_cols = down_weight.shape[0]
    hidden = low(jax.nn.silu(gate_cols[:, :hidden_cols]) * gate_cols[:, hidden_cols:])
    feed_out = low_back(matmul(hidden, down_weight))
    return valid_mask[:, None] * (middle + feed_out)

def reference(tokens, lengths, norm_gain, mixer_in, lower_bound, head_gain, head_merge, feed_gain, gate_up, down_weight, out_grad):
    params = tuple((member.astype(jnp.float32) for member in (norm_gain, mixer_in, lower_bound, head_gain, head_merge, feed_gain, gate_up, down_weight)))
    positions = jnp.arange(tokens.shape[1], dtype=jnp.int32)

    def one_sequence(totals, sequence):
        tokens_row, length_one, grad_row = sequence
        valid_mask = (positions < length_one).astype(jnp.float32)

        def closed(rows_in, *weights):
            return block_forward(rows_in, valid_mask, *weights)
        output, pullback = jax.vjp(closed, tokens_row.astype(jnp.float32), *params)
        gradients = pullback(grad_row.astype(jnp.float32))
        totals = tuple((running + addend for running, addend in zip(totals, gradients[1:])))
        return (totals, (output.astype(jnp.bfloat16), gradients[0].astype(jnp.bfloat16)))
    start_sums = tuple((jnp.zeros_like(member) for member in params))
    totals, stacked = lax.scan(one_sequence, start_sums, (tokens, lengths, out_grad))
    return (stacked[0], stacked[1], totals[0], totals[1], totals[2], totals[3], totals[4], totals[5], totals[6], totals[7])
```

```python
import functools

import jax
import jax.numpy as jnp
import numpy as np
from jax import lax
from jax.experimental import pallas as pl
from jax.experimental.pallas import tpu as pltpu
from jax.sharding import PartitionSpec as P

EPS = 1e-06
CHUNK = 32
BF = jnp.bfloat16
F32 = jnp.float32


def mm(first_mat, second_mat, first_dim, second_dim):
    return lax.dot_general(
        first_mat, second_mat, (((first_dim,), (second_dim,)), ((), ())), preferred_element_type=F32
    )


def split_sum(mask_two, values):
    high = values.astype(BF)
    rest = (values - high.astype(F32)).astype(BF)
    return mm(mask_two, jnp.concatenate([high, rest], axis=0), 1, 0)


def order_masks(size, keep):
    row = lax.broadcasted_iota(jnp.int32, (size, 2 * size), 0)
    col = lax.broadcasted_iota(jnp.int32, (size, 2 * size), 1)
    col = jnp.where(col >= size, col - size, col)
    return keep(row, col).astype(F32).astype(BF)


def causal_of(size):
    row = lax.broadcasted_iota(jnp.int32, (size, size), 0)
    col = lax.broadcasted_iota(jnp.int32, (size, size), 1)
    return col <= row


def gates_of(proj, bound, width):
    query_pre = proj[:, :width]
    sig_query = jax.nn.sigmoid(query_pre)
    sig_forget = jax.nn.sigmoid(proj[:, width : 2 * width])
    forget = bound + (1.0 - bound) * sig_forget
    queries = (query_pre * sig_query).astype(BF).astype(F32)
    keys = (1.0 - forget).astype(BF).astype(F32)
    values = proj[:, 2 * width :].astype(BF)
    return query_pre, sig_query, sig_forget, forget, queries, keys, values


def forward_body(own_ref, proj_ref, bound_ref, gain_ref, mixed_ref, head_ref, states_ref, state_ref):
    seqs = proj_ref.shape[1]
    width = proj_ref.shape[3] // 3
    hd = gain_ref.shape[1]
    heads = width // hd
    mid = CHUNK // 2 - 1

    @pl.when(pl.program_id(0) == 0)
    def _():
        state_ref[...] = jnp.zeros_like(state_ref)

    tri = order_masks(CHUNK, lambda row, col: col <= row)
    causal = causal_of(CHUNK)
    gain = gain_ref[...]
    for seq in range(seqs):
        _, _, _, forget, queries, keys, values = gates_of(proj_ref[0, seq], bound_ref[...], width)
        total = split_sum(tri, jnp.log(forget))
        middle = total[mid : mid + 1]
        end = total[CHUNK - 1 : CHUNK]
        query_near = queries * jnp.exp(total - middle)
        key_near = keys * jnp.exp(middle - total)
        query_far = (query_near * jnp.exp(middle)).astype(BF)
        key_far = (key_near * jnp.exp(end - middle)).astype(BF)
        query_near = query_near.astype(BF)
        key_near = key_near.astype(BF)
        decay = jnp.exp(end)
        for head in range(heads):
            cut = slice(head * hd, (head + 1) * hd)
            at = seq * heads + head
            state = state_ref[at]
            state_low = state.astype(BF)
            states_ref[0, at] = state_low
            scores = mm(query_near[:, cut], key_near[:, cut], 1, 1)
            scores = jnp.where(causal, scores, 0.0).astype(BF)
            mixed = mm(query_far[:, cut], state_low, 1, 1) + mm(scores, values[:, cut], 1, 0)
            state_ref[at] = state * decay[:, cut] + mm(values[:, cut], key_far[:, cut], 0, 0)
            scale = lax.rsqrt(jnp.mean(mixed * mixed, axis=-1, keepdims=True) + EPS)
            mixed_ref[0, seq, :, cut] = mixed
            head_ref[0, seq, :, cut] = (mixed * scale * gain).astype(BF)


def backward_body(
    own_ref,
    proj_ref,
    mixed_ref,
    out_ref,
    states_ref,
    bound_ref,
    gain_ref,
    grad_ref,
    bound_sum_ref,
    head_sum_ref,
    back_ref,
):
    seqs = proj_ref.shape[1]
    width = proj_ref.shape[3] // 3
    hd = gain_ref.shape[1]
    heads = width // hd
    mid = CHUNK // 2 - 1

    @pl.when(pl.program_id(0) == 0)
    def _():
        back_ref[...] = jnp.zeros_like(back_ref)
        bound_sum_ref[...] = jnp.zeros_like(bound_sum_ref)
        head_sum_ref[...] = jnp.zeros_like(head_sum_ref)

    tri = order_masks(CHUNK, lambda row, col: col <= row)
    tri_up = order_masks(CHUNK, lambda row, col: col >= row)
    tri_under = order_masks(CHUNK, lambda row, col: col < row)
    causal = causal_of(CHUNK)
    gain = gain_ref[...]
    bound = bound_ref[...]
    head_sum = jnp.zeros((1, hd), F32)
    bound_sum = jnp.zeros((1, width), F32)
    for seq in range(seqs):
        query_pre, sig_query, sig_forget, forget, queries, keys, values = gates_of(
            proj_ref[0, seq], bound, width
        )
        total = split_sum(tri, jnp.log(forget))
        middle = total[mid : mid + 1]
        end = total[CHUNK - 1 : CHUNK]
        exp_query = jnp.exp(total - middle)
        exp_key = jnp.exp(middle - total)
        query_near_f = queries * exp_query
        key_near_f = keys * exp_key
        exp_mid = jnp.exp(middle)
        exp_rest = jnp.exp(end - middle)
        query_far = (query_near_f * exp_mid).astype(BF)
        key_far = (key_near_f * exp_rest).astype(BF)
        query_near = query_near_f.astype(BF)
        key_near = key_near_f.astype(BF)
        decay = jnp.exp(end)
        later_parts = []
        sooner_parts = []
        edge_parts = []
        query_parts = []
        key_parts = []
        value_parts = []
        for head in range(heads):
            cut = slice(head * hd, (head + 1) * hd)
            at = seq * heads + head
            mixed = mixed_ref[0, seq, :, cut]
            out_head = out_ref[0, seq, :, cut].astype(F32)
            scale = lax.rsqrt(jnp.mean(mixed * mixed, axis=-1, keepdims=True) + EPS)
            weighted = gain * out_head
            along = jnp.mean(weighted * mixed, axis=-1, keepdims=True)
            grad = (scale * weighted - mixed * ((scale * scale * scale) * along)).astype(BF)
            head_sum = head_sum + jnp.sum(out_head * mixed * scale, axis=0, keepdims=True)
            state_low = states_ref[0, at]
            back = back_ref[at]
            back_low = back.astype(BF)
            value = values[:, cut]
            scores = mm(query_near[:, cut], key_near[:, cut], 1, 1)
            scores = jnp.where(causal, scores, 0.0).astype(BF)
            cross = mm(grad, value, 1, 1)
            cross = jnp.where(causal, cross, 0.0).astype(BF)
            query_far_grad = exp_mid[:, cut] * mm(grad, state_low, 1, 0)
            query_near_grad = mm(cross, key_near[:, cut], 1, 0)
            key_far_grad = exp_rest[:, cut] * mm(value, back_low, 1, 0)
            key_near_grad = mm(cross, query_near[:, cut], 0, 0)
            query_low = query_near[:, cut].astype(F32)
            key_low = key_near[:, cut].astype(F32)
            later_parts.append(query_low * (query_far_grad + query_near_grad) - key_low * key_near_grad)
            sooner_parts.append(key_low * key_far_grad)
            edge_parts.append(
                decay[:, cut] * jnp.sum(state_low.astype(F32) * back, axis=0, keepdims=True)
            )
            query_parts.append(exp_query[:, cut] * (query_far_grad + query_near_grad))
            key_parts.append(exp_key[:, cut] * (key_far_grad + key_near_grad))
            value_parts.append(mm(key_far[:, cut], back_low, 1, 1) + mm(scores, grad, 0, 0))
            back_ref[at] = back * decay[:, cut] + mm(grad, query_far[:, cut], 0, 0)
        query_grad = jnp.concatenate(query_parts, axis=1)
        key_grad = jnp.concatenate(key_parts, axis=1)
        log_grad = (
            split_sum(tri_up, jnp.concatenate(later_parts, axis=1))
            + split_sum(tri_under, jnp.concatenate(sooner_parts, axis=1))
            + jnp.concatenate(edge_parts, axis=1)
        )
        forget_grad = log_grad / forget - key_grad
        bound_sum = bound_sum + jnp.sum(forget_grad * (1.0 - sig_forget), axis=0, keepdims=True)
        grad_ref[0, seq, :, :width] = (
            query_grad * sig_query * (1.0 + query_pre * (1.0 - sig_query))
        ).astype(BF)
        grad_ref[0, seq, :, width : 2 * width] = (
            forget_grad * (1.0 - bound) * sig_forget * (1.0 - sig_forget)
        ).astype(BF)
        grad_ref[0, seq, :, 2 * width :] = jnp.concatenate(value_parts, axis=1).astype(BF)
    bound_sum_ref[...] += bound_sum
    head_sum_ref[...] += head_sum


def place_of(chunk, own, per_piece):
    return lax.bitwise_xor(chunk // per_piece, own), chunk % per_piece


def recur_forward(own, proj, bound, gain):
    pieces, seqs, rows, three = proj.shape
    width = three // 3
    hd = gain.shape[1]
    per = rows // CHUNK
    chunks = pieces * per
    many = seqs * width // hd

    def rows_at(chunk, own_ref):
        piece, block = place_of(chunk, own_ref[0], per)
        return (piece, 0, block, 0)

    return pl.pallas_call(
        forward_body,
        grid_spec=pltpu.PrefetchScalarGridSpec(
            num_scalar_prefetch=1,
            grid=(chunks,),
            in_specs=[
                pl.BlockSpec((1, seqs, CHUNK, three), rows_at),
                pl.BlockSpec((1, width), lambda chunk, own_ref: (0, 0)),
                pl.BlockSpec((1, hd), lambda chunk, own_ref: (0, 0)),
            ],
            out_specs=[
                pl.BlockSpec((1, seqs, CHUNK, width), rows_at),
                pl.BlockSpec((1, seqs, CHUNK, width), rows_at),
                pl.BlockSpec((1, many, hd, hd), lambda chunk, own_ref: (chunk, 0, 0, 0)),
            ],
            scratch_shapes=[pltpu.VMEM((many, hd, hd), F32)],
        ),
        out_shape=[
            jax.ShapeDtypeStruct((pieces, seqs, rows, width), F32),
            jax.ShapeDtypeStruct((pieces, seqs, rows, width), BF),
            jax.ShapeDtypeStruct((chunks, many, hd, hd), BF),
        ],
        compiler_params=pltpu.CompilerParams(
            dimension_semantics=("arbitrary",), vmem_limit_bytes=32 * 1024 * 1024
        ),
        name="recur_forward",
    )(own, proj, bound, gain)


def recur_backward(own, proj, mixed, out_head, states, bound, gain):
    pieces, seqs, rows, three = proj.shape
    width = three // 3
    hd = gain.shape[1]
    per = rows // CHUNK
    chunks = pieces * per
    many = seqs * width // hd

    def rows_at(step, own_ref):
        piece, block = place_of(chunks - 1 - step, own_ref[0], per)
        return (piece, 0, block, 0)

    return pl.pallas_call(
        backward_body,
        grid_spec=pltpu.PrefetchScalarGridSpec(
            num_scalar_prefetch=1,
            grid=(chunks,),
            in_specs=[
                pl.BlockSpec((1, seqs, CHUNK, three), rows_at),
                pl.BlockSpec((1, seqs, CHUNK, width), rows_at),
                pl.BlockSpec((1, seqs, CHUNK, width), rows_at),
                pl.BlockSpec((1, many, hd, hd), lambda step, own_ref: (chunks - 1 - step, 0, 0, 0)),
                pl.BlockSpec((1, width), lambda step, own_ref: (0, 0)),
                pl.BlockSpec((1, hd), lambda step, own_ref: (0, 0)),
            ],
            out_specs=[
                pl.BlockSpec((1, seqs, CHUNK, three), rows_at),
                pl.BlockSpec((1, width), lambda step, own_ref: (0, 0)),
                pl.BlockSpec((1, hd), lambda step, own_ref: (0, 0)),
            ],
            scratch_shapes=[pltpu.VMEM((many, hd, hd), F32)],
        ),
        out_shape=[
            jax.ShapeDtypeStruct((pieces, seqs, rows, three), BF),
            jax.ShapeDtypeStruct((1, width), F32),
            jax.ShapeDtypeStruct((1, hd), F32),
        ],
        compiler_params=pltpu.CompilerParams(
            dimension_semantics=("arbitrary",), vmem_limit_bytes=32 * 1024 * 1024
        ),
        name="recur_backward",
    )(own, proj, mixed, out_head, states, bound, gain)


def rms_rows(values, gain_vec):
    scaling = lax.rsqrt(jnp.mean(values * values, axis=-1, keepdims=True) + EPS)
    return values * scaling * gain_vec, scaling


def norm_back(values, scaling, gain_vec, upstream):
    weighted = gain_vec * upstream
    along = jnp.mean(weighted * values, axis=-1, keepdims=True)
    return (
        scaling * weighted - values * (scaling * scaling * scaling) * along,
        upstream * values * scaling,
    )


def assemble_body(count, at_ref, *refs):
    pieces, out_ref, held, in_sems, out_sems = refs[:count], refs[count], *refs[count + 1 :]
    rows = pieces[0].shape[0]
    loads = [pltpu.make_async_copy(pieces[i], held.at[i], in_sems.at[i]) for i in range(count)]
    for load in loads:
        load.start()
    stores = []
    for i in range(count):
        start = pl.multiple_of(at_ref[i] * rows, rows)
        loads[i].wait()
        stores.append(
            pltpu.make_async_copy(held.at[i], out_ref.at[pl.ds(start, rows), :], out_sems.at[i])
        )
        stores[i].start()
    for store in stores:
        store.wait()


def assemble(at, pieces):
    count = len(pieces)
    rows, cols = pieces[0].shape
    if rows % 16:
        whole = jnp.zeros((count * rows, cols), pieces[0].dtype)
        for i, piece in enumerate(pieces):
            whole = lax.dynamic_update_slice_in_dim(whole, piece, at[i] * rows, 0)
        return whole
    return pl.pallas_call(
        functools.partial(assemble_body, count),
        in_specs=[pl.BlockSpec(memory_space=pltpu.SMEM)] + [pl.BlockSpec(memory_space=pl.ANY)] * count,
        out_specs=pl.BlockSpec(memory_space=pl.ANY),
        out_shape=jax.ShapeDtypeStruct((count * rows, cols), pieces[0].dtype),
        scratch_shapes=[
            pltpu.VMEM((count, rows, cols), pieces[0].dtype),
            pltpu.SemaphoreType.DMA((count,)),
            pltpu.SemaphoreType.DMA((count,)),
        ],
        compiler_params=pltpu.CompilerParams(vmem_limit_bytes=32 * 1024 * 1024),
        name="assemble",
    )(at, *pieces)


AXES = ("dp", "tensor")


def make_local(dp_size, tensor_size):
    columns = dp_size // 2
    bits = [1 << i for i in range(columns.bit_length() - 1)]

    def route(step, invert=False):
        pairs = []
        for dp in range(dp_size):
            for z in range(tensor_size):
                col, core, place = step(dp >> 1, dp & 1, z)
                pair = (dp * tensor_size + z, (col * 2 + core) * tensor_size + place)
                pairs.append(pair[::-1] if invert else pair)
        return sorted(pairs)

    def spread(flip):
        return lambda col, core, z: (col, z & 1, 2 * (core ^ flip) + (z >> 1))

    spreads = [route(spread(flip)) for flip in (0, 1)]
    returns = [route(spread(flip), True) for flip in (0, 1)]
    core_swap = route(lambda col, core, z: (col, core ^ 1, z))
    z_swap = route(lambda col, core, z: (col, core, z ^ 1))
    col_swap = {bit: route(lambda col, core, z, bit=bit: (col ^ bit, core, z)) for bit in bits}
    orders = [bits, bits[::-1]]

    def move(array, pairs):
        return lax.ppermute(array, AXES, pairs)

    def sum_all(array):
        total = dp_size * tensor_size
        for step in range(total.bit_length() - 1):
            array = array + move(array, [(at, at ^ (1 << step)) for at in range(total)])
        return array

    def gather_weight(shard, places):
        pieces = []
        spots = []
        for half in range(2):
            held = [(0, move(shard, spreads[half]))]
            for bit in orders[half]:
                held = held + [(at ^ bit, move(piece, col_swap[bit])) for at, piece in held]
            for at, piece in held:
                pieces.append(piece)
                spots.append(places(at, half))
        return assemble(jnp.stack(spots).astype(jnp.int32), pieces)

    def scatter_grad(piece_of):
        total = None
        for half in range(2):
            held = {at: piece_of(at, half) for at in range(columns)}
            for bit in orders[half][::-1]:
                for at in sorted(held):
                    if at & bit:
                        arrived = move(held.pop(at), col_swap[bit])
                        held[at ^ bit] = (
                            held[at ^ bit].astype(F32) + arrived.astype(F32)
                        ).astype(BF)
            back = move(held[0], returns[half]).astype(F32)
            total = back if total is None else total + back
        return total

    def gather_rows(own):
        near = move(own, core_swap)
        far = move(own, z_swap)
        return jnp.stack([own, near, far, move(far, core_swap)])

    def scatter_rows(far_pair, own_pair):
        far = far_pair[0].astype(F32) + move(far_pair[1], core_swap).astype(F32)
        far = move(far.astype(BF), z_swap)
        return own_pair[0].astype(F32) + move(own_pair[1], core_swap).astype(F32) + far.astype(F32)

    def split_rows(compute, *arrays):
        half = arrays[0].shape[0] // 2
        return [compute(*(array[at:to] for array in arrays)) for at, to in ((half, 2 * half), (0, half))]

    def dot_rows(first_mat, second_mat, second_dim):
        return lax.dot_general(
            first_mat,
            second_mat,
            (((first_mat.ndim - 1,), (second_dim,)), ((), ())),
            preferred_element_type=F32,
        )

    def local(
        tokens,
        lengths,
        norm_gain,
        mixer_in,
        lower_bound,
        head_gain,
        head_merge,
        feed_gain,
        gate_up,
        down_weight,
        out_grad,
    ):
        seqs, rows, model = tokens.shape
        dp_at = lax.axis_index("dp")
        z_at = lax.axis_index("tensor")
        col = dp_at // 2
        half_at = z_at // 2
        role = 2 * (z_at % 2) + dp_at % 2

        def places(at, half):
            return lax.bitwise_xor(col, at) * 2 + (half_at if half == 0 else 1 - half_at)

        lens = move(lengths, spreads[0])
        tok = move(tokens, spreads[0])
        mixer_mat = gather_weight(mixer_in.reshape(mixer_in.shape[0], -1), places)
        merge_mat = gather_weight(head_merge, places)
        gates_mat = gather_weight(gate_up.reshape(gate_up.shape[0], -1), places)
        down_mat = gather_weight(down_weight, places)
        out_rows = move(out_grad, spreads[0])

        vectors = [norm_gain, feed_gain, head_gain, lower_bound]
        vector_ends = np.cumsum([vector.shape[0] for vector in vectors])
        packed = jnp.zeros((dp_size * tensor_size, vector_ends[-1]), BF)
        packed = lax.dynamic_update_slice_in_dim(
            packed, jnp.concatenate(vectors)[None], dp_at * tensor_size + z_at, 0
        )
        packed = sum_all(packed).reshape(dp_size, tensor_size, -1).astype(F32)
        norm_vec = packed[:, 0, : vector_ends[0]].reshape(-1)
        feed_vec = packed[:, 0, vector_ends[0] : vector_ends[1]].reshape(-1)
        head_vec = packed[:, 0, vector_ends[1] : vector_ends[2]].reshape(1, -1)
        bound_vec = lax.dynamic_index_in_dim(packed, role, 1, False)[:, vector_ends[2] :].reshape(1, -1)

        positions = role * rows + jnp.arange(rows, dtype=jnp.int32)
        valid = (positions[None, :] < lens[:, None]).astype(F32)[:, :, None]
        own = role.astype(jnp.int32).reshape(1)

        masked = tok.astype(F32) * valid
        normed, scale_one = rms_rows(masked, norm_vec)
        first_in = gather_rows(normed.astype(BF))
        projected = dot_rows(first_in, mixer_mat, 0)
        mixed, head_out, states = recur_forward(own, projected, bound_vec, head_vec)
        attn = scatter_rows(*split_rows(lambda part: dot_rows(part, merge_mat, 0).astype(BF), head_out))
        middle = masked + attn
        normed_two, scale_two = rms_rows(middle, feed_vec)
        second_in = gather_rows(normed_two.astype(BF))
        gate_pre = dot_rows(second_in, gates_mat, 0)
        hidden_cols = down_mat.shape[0]
        gate_part = gate_pre[..., :hidden_cols]
        up_part = gate_pre[..., hidden_cols:]
        sig_gate = jax.nn.sigmoid(gate_part)
        hidden = (gate_part * sig_gate * up_part).astype(BF)
        feed_out = scatter_rows(*split_rows(lambda part: dot_rows(part, down_mat, 0).astype(BF), hidden))
        block_out = move((valid * (middle + feed_out)).astype(BF), returns[0])

        upstream = out_rows.astype(F32) * valid
        branch_in = gather_rows(upstream.astype(BF))
        hidden_grad = dot_rows(branch_in, down_mat, 1)
        gate_grad = hidden_grad * up_part * sig_gate * (1.0 + gate_part * (1.0 - sig_gate))
        up_grad = hidden_grad * gate_part * sig_gate
        both_grad = jnp.concatenate([gate_grad, up_grad], axis=-1).astype(BF)
        second_grad = scatter_rows(
            *split_rows(lambda part: dot_rows(part, gates_mat, 1).astype(BF), both_grad)
        )
        middle_grad, feed_terms = norm_back(middle, scale_two, feed_vec, second_grad)
        middle_grad = middle_grad + upstream
        attn_in = gather_rows(middle_grad.astype(BF))
        out_head = dot_rows(attn_in, merge_mat, 1)
        proj_grad, bound_sum, head_sum = recur_backward(
            own, projected, mixed, out_head, states, bound_vec, head_vec
        )
        first_grad = scatter_rows(
            *split_rows(lambda part: dot_rows(part, mixer_mat, 1).astype(BF), proj_grad)
        )
        masked_grad, norm_terms = norm_back(masked, scale_one, norm_vec, first_grad)
        input_grad = move((valid * (masked_grad + middle_grad)).astype(BF), returns[0])

        def weight_grad(first_mat, second_mat):
            return lax.dot_general(
                first_mat.reshape(-1, first_mat.shape[-1]),
                second_mat.reshape(-1, second_mat.shape[-1]),
                (((0,), (0,)), ((), ())),
                preferred_element_type=F32,
            ).astype(BF)

        def by_rows(whole, count):
            return lambda at, half: lax.dynamic_slice_in_dim(whole, places(at, half) * count, count, 0)

        down_grad = scatter_grad(by_rows(weight_grad(hidden, branch_in), down_weight.shape[0]))
        gates_grad = scatter_grad(by_rows(weight_grad(second_in, both_grad), gate_up.shape[0]))
        merge_grad = scatter_grad(by_rows(weight_grad(head_out, attn_in), head_merge.shape[0]))
        mixer_grad = scatter_grad(by_rows(weight_grad(first_in, proj_grad), mixer_in.shape[0]))

        bound_all = jnp.zeros((tensor_size, bound_sum.shape[1]), F32)
        bound_all = lax.dynamic_update_slice_in_dim(bound_all, bound_sum, role, 0)
        sums = [
            jnp.sum(norm_terms, axis=(0, 1)),
            jnp.sum(feed_terms, axis=(0, 1)),
            head_sum.reshape(-1),
            bound_all.reshape(-1),
        ]
        ends = np.cumsum([part.shape[0] for part in sums])
        summed = sum_all(jnp.concatenate(sums))

        def shard_of(vector, count, at):
            return lax.dynamic_slice_in_dim(vector, at * count, count, 0)

        return (
            block_out,
            input_grad,
            shard_of(summed[: ends[0]], norm_gain.shape[0], dp_at),
            mixer_grad.reshape(mixer_in.shape),
            shard_of(summed[ends[2] :], lower_bound.shape[0], z_at * dp_size + dp_at),
            shard_of(summed[ends[1] : ends[2]], head_gain.shape[0], dp_at),
            merge_grad,
            shard_of(summed[ends[0] : ends[1]], feed_gain.shape[0], dp_at),
            gates_grad.reshape(gate_up.shape),
            down_grad,
        )

    return local


def solution(mesh):
    rows_spec = P("dp", "tensor", None)
    wide_spec = P("dp", None, "tensor")
    tall_spec = P(("tensor", "dp"), None)
    return jax.shard_map(
        make_local(mesh.shape["dp"], mesh.shape["tensor"]),
        mesh=mesh,
        in_specs=(
            rows_spec,
            P("dp"),
            P("dp"),
            wide_spec,
            P(("tensor", "dp")),
            P("dp"),
            tall_spec,
            P("dp"),
            wide_spec,
            tall_spec,
            rows_spec,
        ),
        out_specs=(
            rows_spec,
            rows_spec,
            P("dp"),
            wide_spec,
            P(("tensor", "dp")),
            P("dp"),
            tall_spec,
            P("dp"),
            wide_spec,
            tall_spec,
        ),
        check_vma=False,
    )
```

```python
import functools

import jax
import jax.numpy as jnp
import numpy as np
from jax import lax
from jax.experimental import pallas as pl
from jax.experimental.pallas import tpu as pltpu
from jax.sharding import PartitionSpec as P

EPS = 1e-06
CHUNK = 32
BF = jnp.bfloat16
F32 = jnp.float32


def mm(first_mat, second_mat, first_dim, second_dim):
    return lax.dot_general(
        first_mat, second_mat, (((first_dim,), (second_dim,)), ((), ())), preferred_element_type=F32
    )


def split_sum(mask_two, values):
    high = values.astype(BF)
    rest = (values - high.astype(F32)).astype(BF)
    return mm(mask_two, jnp.concatenate([high, rest], axis=0), 1, 0)


def order_masks(size, keep):
    row = lax.broadcasted_iota(jnp.int32, (size, 2 * size), 0)
    col = lax.broadcasted_iota(jnp.int32, (size, 2 * size), 1)
    col = jnp.where(col >= size, col - size, col)
    return keep(row, col).astype(F32).astype(BF)


def causal_of(size):
    row = lax.broadcasted_iota(jnp.int32, (size, size), 0)
    col = lax.broadcasted_iota(jnp.int32, (size, size), 1)
    return col <= row


def gates_of(proj, bound, width):
    query_pre = proj[:, :width]
    sig_query = jax.nn.sigmoid(query_pre)
    sig_forget = jax.nn.sigmoid(proj[:, width : 2 * width])
    forget = bound + (1.0 - bound) * sig_forget
    queries = (query_pre * sig_query).astype(BF).astype(F32)
    keys = (1.0 - forget).astype(BF).astype(F32)
    values = proj[:, 2 * width :].astype(BF)
    return query_pre, sig_query, sig_forget, forget, queries, keys, values


def forward_body(own_ref, proj_ref, bound_ref, gain_ref, mixed_ref, head_ref, states_ref, state_ref):
    seqs = proj_ref.shape[1]
    width = proj_ref.shape[3] // 3
    hd = gain_ref.shape[1]
    heads = width // hd
    mid = CHUNK // 2 - 1

    @pl.when(pl.program_id(0) == 0)
    def _():
        state_ref[...] = jnp.zeros_like(state_ref)

    tri = order_masks(CHUNK, lambda row, col: col <= row)
    causal = causal_of(CHUNK)
    gain = gain_ref[...]
    for seq in range(seqs):
        _, _, _, forget, queries, keys, values = gates_of(proj_ref[0, seq], bound_ref[...], width)
        total = split_sum(tri, jnp.log(forget))
        middle = total[mid : mid + 1]
        end = total[CHUNK - 1 : CHUNK]
        query_near = queries * jnp.exp(total - middle)
        key_near = keys * jnp.exp(middle - total)
        query_far = (query_near * jnp.exp(middle)).astype(BF)
        key_far = (key_near * jnp.exp(end - middle)).astype(BF)
        query_near = query_near.astype(BF)
        key_near = key_near.astype(BF)
        decay = jnp.exp(end)
        for head in range(heads):
            cut = slice(head * hd, (head + 1) * hd)
            at = seq * heads + head
            state = state_ref[at]
            state_low = state.astype(BF)
            states_ref[0, at] = state_low
            scores = mm(query_near[:, cut], key_near[:, cut], 1, 1)
            scores = jnp.where(causal, scores, 0.0).astype(BF)
            mixed = mm(query_far[:, cut], state_low, 1, 1) + mm(scores, values[:, cut], 1, 0)
            state_ref[at] = state * decay[:, cut] + mm(values[:, cut], key_far[:, cut], 0, 0)
            scale = lax.rsqrt(jnp.mean(mixed * mixed, axis=-1, keepdims=True) + EPS)
            mixed_ref[0, seq, :, cut] = mixed
            head_ref[0, seq, :, cut] = (mixed * scale * gain).astype(BF)


def backward_body(
    own_ref,
    proj_ref,
    mixed_ref,
    out_ref,
    states_ref,
    bound_ref,
    gain_ref,
    grad_ref,
    bound_sum_ref,
    head_sum_ref,
    back_ref,
):
    seqs = proj_ref.shape[1]
    width = proj_ref.shape[3] // 3
    hd = gain_ref.shape[1]
    heads = width // hd
    mid = CHUNK // 2 - 1

    @pl.when(pl.program_id(0) == 0)
    def _():
        back_ref[...] = jnp.zeros_like(back_ref)
        bound_sum_ref[...] = jnp.zeros_like(bound_sum_ref)
        head_sum_ref[...] = jnp.zeros_like(head_sum_ref)

    tri = order_masks(CHUNK, lambda row, col: col <= row)
    tri_up = order_masks(CHUNK, lambda row, col: col >= row)
    tri_under = order_masks(CHUNK, lambda row, col: col < row)
    causal = causal_of(CHUNK)
    gain = gain_ref[...]
    bound = bound_ref[...]
    head_sum = jnp.zeros((1, hd), F32)
    bound_sum = jnp.zeros((1, width), F32)
    for seq in range(seqs):
        query_pre, sig_query, sig_forget, forget, queries, keys, values = gates_of(
            proj_ref[0, seq], bound, width
        )
        total = split_sum(tri, jnp.log(forget))
        middle = total[mid : mid + 1]
        end = total[CHUNK - 1 : CHUNK]
        exp_query = jnp.exp(total - middle)
        exp_key = jnp.exp(middle - total)
        query_near_f = queries * exp_query
        key_near_f = keys * exp_key
        exp_mid = jnp.exp(middle)
        exp_rest = jnp.exp(end - middle)
        query_far = (query_near_f * exp_mid).astype(BF)
        key_far = (key_near_f * exp_rest).astype(BF)
        query_near = query_near_f.astype(BF)
        key_near = key_near_f.astype(BF)
        decay = jnp.exp(end)
        later_parts = []
        sooner_parts = []
        edge_parts = []
        query_parts = []
        key_parts = []
        value_parts = []
        for head in range(heads):
            cut = slice(head * hd, (head + 1) * hd)
            at = seq * heads + head
            mixed = mixed_ref[0, seq, :, cut]
            out_head = out_ref[0, seq, :, cut].astype(F32)
            scale = lax.rsqrt(jnp.mean(mixed * mixed, axis=-1, keepdims=True) + EPS)
            weighted = gain * out_head
            along = jnp.mean(weighted * mixed, axis=-1, keepdims=True)
            grad = (scale * weighted - mixed * ((scale * scale * scale) * along)).astype(BF)
            head_sum = head_sum + jnp.sum(out_head * mixed * scale, axis=0, keepdims=True)
            state_low = states_ref[0, at]
            back = back_ref[at]
            back_low = back.astype(BF)
            value = values[:, cut]
            scores = mm(query_near[:, cut], key_near[:, cut], 1, 1)
            scores = jnp.where(causal, scores, 0.0).astype(BF)
            cross = mm(grad, value, 1, 1)
            cross = jnp.where(causal, cross, 0.0).astype(BF)
            query_far_grad = exp_mid[:, cut] * mm(grad, state_low, 1, 0)
            query_near_grad = mm(cross, key_near[:, cut], 1, 0)
            key_far_grad = exp_rest[:, cut] * mm(value, back_low, 1, 0)
            key_near_grad = mm(cross, query_near[:, cut], 0, 0)
            query_low = query_near[:, cut].astype(F32)
            key_low = key_near[:, cut].astype(F32)
            later_parts.append(query_low * (query_far_grad + query_near_grad) - key_low * key_near_grad)
            sooner_parts.append(key_low * key_far_grad)
            edge_parts.append(
                decay[:, cut] * jnp.sum(state_low.astype(F32) * back, axis=0, keepdims=True)
            )
            query_parts.append(exp_query[:, cut] * (query_far_grad + query_near_grad))
            key_parts.append(exp_key[:, cut] * (key_far_grad + key_near_grad))
            value_parts.append(mm(key_far[:, cut], back_low, 1, 1) + mm(scores, grad, 0, 0))
            back_ref[at] = back * decay[:, cut] + mm(grad, query_far[:, cut], 0, 0)
        query_grad = jnp.concatenate(query_parts, axis=1)
        key_grad = jnp.concatenate(key_parts, axis=1)
        log_grad = (
            split_sum(tri_up, jnp.concatenate(later_parts, axis=1))
            + split_sum(tri_under, jnp.concatenate(sooner_parts, axis=1))
            + jnp.concatenate(edge_parts, axis=1)
        )
        forget_grad = log_grad / forget - key_grad
        bound_sum = bound_sum + jnp.sum(forget_grad * (1.0 - sig_forget), axis=0, keepdims=True)
        grad_ref[0, seq, :, :width] = (
            query_grad * sig_query * (1.0 + query_pre * (1.0 - sig_query))
        ).astype(BF)
        grad_ref[0, seq, :, width : 2 * width] = (
            forget_grad * (1.0 - bound) * sig_forget * (1.0 - sig_forget)
        ).astype(BF)
        grad_ref[0, seq, :, 2 * width :] = jnp.concatenate(value_parts, axis=1).astype(BF)
    bound_sum_ref[...] += bound_sum
    head_sum_ref[...] += head_sum


def place_of(chunk, own, per_piece):
    return lax.bitwise_xor(chunk // per_piece, own), chunk % per_piece


def recur_forward(own, proj, bound, gain):
    pieces, seqs, rows, three = proj.shape
    width = three // 3
    hd = gain.shape[1]
    per = rows // CHUNK
    chunks = pieces * per
    many = seqs * width // hd

    def rows_at(chunk, own_ref):
        piece, block = place_of(chunk, own_ref[0], per)
        return (piece, 0, block, 0)

    return pl.pallas_call(
        forward_body,
        grid_spec=pltpu.PrefetchScalarGridSpec(
            num_scalar_prefetch=1,
            grid=(chunks,),
            in_specs=[
                pl.BlockSpec((1, seqs, CHUNK, three), rows_at),
                pl.BlockSpec((1, width), lambda chunk, own_ref: (0, 0)),
                pl.BlockSpec((1, hd), lambda chunk, own_ref: (0, 0)),
            ],
            out_specs=[
                pl.BlockSpec((1, seqs, CHUNK, width), rows_at),
                pl.BlockSpec((1, seqs, CHUNK, width), rows_at),
                pl.BlockSpec((1, many, hd, hd), lambda chunk, own_ref: (chunk, 0, 0, 0)),
            ],
            scratch_shapes=[pltpu.VMEM((many, hd, hd), F32)],
        ),
        out_shape=[
            jax.ShapeDtypeStruct((pieces, seqs, rows, width), F32),
            jax.ShapeDtypeStruct((pieces, seqs, rows, width), BF),
            jax.ShapeDtypeStruct((chunks, many, hd, hd), BF),
        ],
        compiler_params=pltpu.CompilerParams(
            dimension_semantics=("arbitrary",), vmem_limit_bytes=32 * 1024 * 1024
        ),
        cost_estimate=pl.CostEstimate(flops=1, bytes_accessed=1, transcendentals=0),
        name="recur_forward",
    )(own, proj, bound, gain)


def recur_backward(own, proj, mixed, out_head, states, bound, gain):
    pieces, seqs, rows, three = proj.shape
    width = three // 3
    hd = gain.shape[1]
    per = rows // CHUNK
    chunks = pieces * per
    many = seqs * width // hd

    def rows_at(step, own_ref):
        piece, block = place_of(chunks - 1 - step, own_ref[0], per)
        return (piece, 0, block, 0)

    return pl.pallas_call(
        backward_body,
        grid_spec=pltpu.PrefetchScalarGridSpec(
            num_scalar_prefetch=1,
            grid=(chunks,),
            in_specs=[
                pl.BlockSpec((1, seqs, CHUNK, three), rows_at),
                pl.BlockSpec((1, seqs, CHUNK, width), rows_at),
                pl.BlockSpec((1, seqs, CHUNK, width), rows_at),
                pl.BlockSpec((1, many, hd, hd), lambda step, own_ref: (chunks - 1 - step, 0, 0, 0)),
                pl.BlockSpec((1, width), lambda step, own_ref: (0, 0)),
                pl.BlockSpec((1, hd), lambda step, own_ref: (0, 0)),
            ],
            out_specs=[
                pl.BlockSpec((1, seqs, CHUNK, three), rows_at),
                pl.BlockSpec((1, width), lambda step, own_ref: (0, 0)),
                pl.BlockSpec((1, hd), lambda step, own_ref: (0, 0)),
            ],
            scratch_shapes=[pltpu.VMEM((many, hd, hd), F32)],
        ),
        out_shape=[
            jax.ShapeDtypeStruct((pieces, seqs, rows, three), BF),
            jax.ShapeDtypeStruct((1, width), F32),
            jax.ShapeDtypeStruct((1, hd), F32),
        ],
        compiler_params=pltpu.CompilerParams(
            dimension_semantics=("arbitrary",), vmem_limit_bytes=32 * 1024 * 1024
        ),
        cost_estimate=pl.CostEstimate(flops=1, bytes_accessed=1, transcendentals=0),
        name="recur_backward",
    )(own, proj, mixed, out_head, states, bound, gain)


def rms_rows(values, gain_vec):
    scaling = lax.rsqrt(jnp.mean(values * values, axis=-1, keepdims=True) + EPS)
    return values * scaling * gain_vec, scaling


def norm_back(values, scaling, gain_vec, upstream):
    weighted = gain_vec * upstream
    along = jnp.mean(weighted * values, axis=-1, keepdims=True)
    return (
        scaling * weighted - values * (scaling * scaling * scaling) * along,
        upstream * values * scaling,
    )


AXES = ("dp", "tensor")


def make_local(dp_size, tensor_size):
    columns = dp_size // 2
    groups = [[2 * col + core for col in range(columns)] for core in range(2)]

    def route(step, invert=False):
        pairs = []
        for dp in range(dp_size):
            for z in range(tensor_size):
                col, core, place = step(dp >> 1, dp & 1, z)
                pair = (dp * tensor_size + z, (col * 2 + core) * tensor_size + place)
                pairs.append(pair[::-1] if invert else pair)
        return sorted(pairs)

    def spread(flip):
        return lambda col, core, z: (col, z & 1, 2 * (core ^ flip) + (z >> 1))

    spreads = [route(spread(flip)) for flip in (0, 1)]
    returns = [route(spread(flip), True) for flip in (0, 1)]
    core_swap = route(lambda col, core, z: (col, core ^ 1, z))
    z_swap = route(lambda col, core, z: (col, core, z ^ 1))

    def move(array, pairs):
        return lax.ppermute(array, AXES, pairs)

    def sum_steps(array, steps):
        total = dp_size * tensor_size
        for step in steps:
            array = array + move(array, [(at, at ^ (1 << step)) for at in range(total)])
        return array

    low_steps = range(tensor_size.bit_length() - 1)
    high_steps = range(tensor_size.bit_length() - 1, (dp_size * tensor_size).bit_length() - 1)

    def after(array, *earlier):
        return lax.optimization_barrier((array, *earlier))[0]

    def ordered(first, second, swap):
        return jnp.where(swap, second, first), jnp.where(swap, first, second)

    def spread_weight(shard):
        return move(shard, spreads[0]), move(shard, spreads[1])

    def joined(pair, swap):
        return jnp.concatenate(ordered(*pair, swap), axis=0)

    def gather_weight(pair):
        return lax.all_gather(pair, "dp", axis=0, tiled=True, axis_index_groups=groups)

    def scatter_grad(whole):
        return lax.psum_scatter(
            whole, "dp", scatter_dimension=0, tiled=True, axis_index_groups=groups
        )

    def return_grad(pair, swap):
        rows = pair.shape[0] // 2
        first, second = ordered(pair[:rows], pair[rows:], swap)
        return move(first, returns[0]).astype(F32) + move(second, returns[1]).astype(F32)

    def gather_rows(own):
        near = move(own, core_swap)
        far = move(own, z_swap)
        return jnp.stack([own, near, far, move(far, core_swap)])

    def scatter_far(far_pair):
        return (far_pair[0].astype(F32) + move(far_pair[1], core_swap).astype(F32)).astype(BF)

    def scatter_own(far, own_pair):
        near = own_pair[0].astype(F32) + move(own_pair[1], core_swap).astype(F32)
        return near + move(far, z_swap).astype(F32)

    def scatter_rows(far_pair, own_pair):
        return scatter_own(scatter_far(far_pair), own_pair)

    def split_rows(compute, *arrays):
        half = arrays[0].shape[0] // 2
        return [compute(*(array[at:to] for array in arrays)) for at, to in ((half, 2 * half), (0, half))]

    def dot_rows(first_mat, second_mat, second_dim):
        return lax.dot_general(
            first_mat,
            second_mat,
            (((first_mat.ndim - 1,), (second_dim,)), ((), ())),
            preferred_element_type=F32,
        )

    def local(
        tokens,
        lengths,
        norm_gain,
        mixer_in,
        lower_bound,
        head_gain,
        head_merge,
        feed_gain,
        gate_up,
        down_weight,
        out_grad,
    ):
        seqs, rows, model = tokens.shape
        dp_at = lax.axis_index("dp")
        z_at = lax.axis_index("tensor")
        half_at = z_at // 2
        role = 2 * (z_at % 2) + dp_at % 2

        def weight_grad(first_mat, second_mat):
            return lax.dot_general(
                first_mat.reshape(-1, first_mat.shape[-1]),
                second_mat.reshape(-1, second_mat.shape[-1]),
                (((0,), (0,)), ((), ())),
                preferred_element_type=F32,
            ).astype(BF)

        swap = half_at == 1
        lens = move(lengths, spreads[0])
        mixer_pair = spread_weight(mixer_in.reshape(mixer_in.shape[0], -1))
        vectors = [norm_gain, feed_gain, head_gain, lower_bound]
        vector_ends = np.cumsum([vector.shape[0] for vector in vectors])
        packed = jnp.zeros((dp_size, vector_ends[-1]), BF)
        packed = lax.dynamic_update_slice_in_dim(packed, jnp.concatenate(vectors)[None], dp_at, 0)
        packed = sum_steps(packed, high_steps)
        tok = move(after(tokens, packed), spreads[0])
        merge_pair = spread_weight(after(head_merge, tok))

        bounds = jnp.zeros((tensor_size, dp_size, lower_bound.shape[0]), BF)
        bounds = lax.dynamic_update_slice_in_dim(bounds, packed[None, :, vector_ends[2] :], z_at, 0)
        bounds = sum_steps(bounds, low_steps)
        vector_rows = packed.astype(F32)
        norm_vec = vector_rows[:, : vector_ends[0]].reshape(-1)
        feed_vec = vector_rows[:, vector_ends[0] : vector_ends[1]].reshape(-1)
        head_vec = vector_rows[:, vector_ends[1] : vector_ends[2]].reshape(1, -1)
        bound_vec = lax.dynamic_index_in_dim(bounds, role, 0, False).astype(F32).reshape(1, -1)

        positions = role * rows + jnp.arange(rows, dtype=jnp.int32)
        valid = (positions[None, :] < lens[:, None]).astype(F32)[:, :, None]
        own = role.astype(jnp.int32).reshape(1)

        masked = tok.astype(F32) * valid
        normed, scale_one = rms_rows(masked, norm_vec)
        normed = normed.astype(BF)
        gates_pair = spread_weight(after(gate_up.reshape(gate_up.shape[0], -1), normed, *merge_pair))
        down_pair = spread_weight(after(down_weight, *gates_pair))
        out_rows = move(after(out_grad, *down_pair), spreads[0])
        mixer_mat = gather_weight(joined(mixer_pair, swap))
        merge_mat = gather_weight(joined(merge_pair, swap))
        first_in = gather_rows(normed)
        gates_mat = gather_weight(joined([after(part, first_in) for part in gates_pair], swap))
        down_mat = gather_weight(joined(down_pair, swap))
        projected = dot_rows(first_in, mixer_mat, 0)
        mixed, head_out, states = recur_forward(own, projected, bound_vec, head_vec)
        attn = scatter_rows(*split_rows(lambda part: dot_rows(part, merge_mat, 0).astype(BF), head_out))
        middle = masked + attn
        normed_two, scale_two = rms_rows(middle, feed_vec)
        upstream = out_rows.astype(F32) * valid
        branch_in = gather_rows(upstream.astype(BF))
        second_in = after(gather_rows(normed_two.astype(BF)), branch_in)
        gate_pre = dot_rows(second_in, gates_mat, 0)
        hidden_cols = down_mat.shape[0]
        gate_part = gate_pre[..., :hidden_cols]
        up_part = gate_pre[..., hidden_cols:]
        sig_gate = jax.nn.sigmoid(gate_part)
        hidden = (gate_part * sig_gate * up_part).astype(BF)
        down_whole = weight_grad(hidden, branch_in)
        down_pair = scatter_grad(down_whole)
        down_grad = return_grad(down_pair, swap)
        hidden_grad = dot_rows(after(branch_in, down_whole), down_mat, 1)
        gate_grad = hidden_grad * up_part * sig_gate * (1.0 + gate_part * (1.0 - sig_gate))
        up_grad = hidden_grad * gate_part * sig_gate
        both_grad = jnp.concatenate([gate_grad, up_grad], axis=-1).astype(BF)
        second_parts = split_rows(lambda part: dot_rows(part, gates_mat, 1).astype(BF), both_grad)
        second_far = scatter_far(second_parts[0])
        second_grad = scatter_own(second_far, second_parts[1])
        gates_whole = weight_grad(second_in, after(both_grad, second_far, *second_parts))
        second_grad = after(second_grad, gates_whole)
        middle_grad, feed_terms = norm_back(middle, scale_two, feed_vec, second_grad)
        middle_grad = middle_grad + upstream
        feed_parts = split_rows(lambda part: dot_rows(part, down_mat, 0).astype(BF), hidden)
        attn_in = after(gather_rows(middle_grad.astype(BF)), *feed_parts)
        feed_out = scatter_rows(*feed_parts)
        block_out = move((valid * (middle + feed_out)).astype(BF), returns[0])
        out_head = dot_rows(after(attn_in, down_grad), merge_mat, 1)
        proj_grad, bound_sum, head_sum = recur_backward(
            own, projected, mixed, out_head, states, bound_vec, head_vec
        )
        first_parts = split_rows(lambda part: dot_rows(part, mixer_mat, 1).astype(BF), proj_grad)
        first_grad = scatter_rows(*first_parts)
        merge_whole = weight_grad(head_out, attn_in)
        mixer_whole = weight_grad(first_in, proj_grad)
        first_grad = after(first_grad, merge_whole, mixer_whole)
        masked_grad, norm_terms = norm_back(masked, scale_one, norm_vec, first_grad)
        input_grad = move((valid * (masked_grad + middle_grad)).astype(BF), returns[0])

        gates_pair = scatter_grad(after(gates_whole, down_pair))
        mixer_pair = scatter_grad(after(mixer_whole, gates_pair, *first_parts))
        merge_pair = scatter_grad(after(merge_whole, mixer_pair))
        gates_grad = return_grad(gates_pair, swap)
        merge_grad = return_grad(merge_pair, swap)
        mixer_grad = return_grad(mixer_pair, swap)

        bound_all = jnp.zeros((tensor_size, bound_sum.shape[1]), F32)
        bound_all = lax.dynamic_update_slice_in_dim(bound_all, bound_sum, role, 0)
        sums = [
            jnp.sum(norm_terms, axis=(0, 1)),
            jnp.sum(feed_terms, axis=(0, 1)),
            head_sum.reshape(-1),
            bound_all.reshape(-1),
        ]
        ends = np.cumsum([part.shape[0] for part in sums])
        summed = sum_steps(after(jnp.concatenate(sums), down_grad, gates_grad), [*low_steps, *high_steps])

        def shard_of(vector, count, at):
            return lax.dynamic_slice_in_dim(vector, at * count, count, 0)

        return (
            block_out,
            input_grad,
            shard_of(summed[: ends[0]], norm_gain.shape[0], dp_at),
            mixer_grad.reshape(mixer_in.shape),
            shard_of(summed[ends[2] :], lower_bound.shape[0], z_at * dp_size + dp_at),
            shard_of(summed[ends[1] : ends[2]], head_gain.shape[0], dp_at),
            merge_grad,
            shard_of(summed[ends[0] : ends[1]], feed_gain.shape[0], dp_at),
            gates_grad.reshape(gate_up.shape),
            down_grad,
        )

    return local


def solution(mesh):
    rows_spec = P("dp", "tensor", None)
    wide_spec = P("dp", None, "tensor")
    tall_spec = P(("tensor", "dp"), None)
    return jax.shard_map(
        make_local(mesh.shape["dp"], mesh.shape["tensor"]),
        mesh=mesh,
        in_specs=(
            rows_spec,
            P("dp"),
            P("dp"),
            wide_spec,
            P(("tensor", "dp")),
            P("dp"),
            tall_spec,
            P("dp"),
            wide_spec,
            tall_spec,
            rows_spec,
        ),
        out_specs=(
            rows_spec,
            rows_spec,
            P("dp"),
            wide_spec,
            P(("tensor", "dp")),
            P("dp"),
            tall_spec,
            P("dp"),
            wide_spec,
            tall_spec,
        ),
        check_vma=False,
    )
```

```python
import functools

import jax
import jax.numpy as jnp
import numpy as np
from jax import lax
from jax.experimental import pallas as pl
from jax.experimental.pallas import tpu as pltpu
from jax.sharding import PartitionSpec as P

EPS = 1e-06
CHUNK = 32
BF = jnp.bfloat16
F32 = jnp.float32


def mm(first_mat, second_mat, first_dim, second_dim):
    return lax.dot_general(
        first_mat, second_mat, (((first_dim,), (second_dim,)), ((), ())), preferred_element_type=F32
    )


def split_sum(mask_two, values):
    high = values.astype(BF)
    rest = (values - high.astype(F32)).astype(BF)
    return mm(mask_two, jnp.concatenate([high, rest], axis=0), 1, 0)


def order_masks(size, keep):
    row = lax.broadcasted_iota(jnp.int32, (size, 2 * size), 0)
    col = lax.broadcasted_iota(jnp.int32, (size, 2 * size), 1)
    col = jnp.where(col >= size, col - size, col)
    return keep(row, col).astype(F32).astype(BF)


def causal_of(size):
    row = lax.broadcasted_iota(jnp.int32, (size, size), 0)
    col = lax.broadcasted_iota(jnp.int32, (size, size), 1)
    return col <= row


def gates_of(proj, bound, width):
    query_pre = proj[:, :width]
    sig_query = jax.nn.sigmoid(query_pre)
    sig_forget = jax.nn.sigmoid(proj[:, width : 2 * width])
    forget = bound + (1.0 - bound) * sig_forget
    queries = (query_pre * sig_query).astype(BF).astype(F32)
    keys = (1.0 - forget).astype(BF).astype(F32)
    values = proj[:, 2 * width :].astype(BF)
    return query_pre, sig_query, sig_forget, forget, queries, keys, values


def forward_body(own_ref, proj_ref, bound_ref, gain_ref, mixed_ref, head_ref, states_ref, state_ref):
    seqs = proj_ref.shape[1]
    width = proj_ref.shape[3] // 3
    hd = gain_ref.shape[1]
    heads = width // hd
    mid = CHUNK // 2 - 1

    @pl.when(pl.program_id(0) == 0)
    def _():
        state_ref[...] = jnp.zeros_like(state_ref)

    tri = order_masks(CHUNK, lambda row, col: col <= row)
    causal = causal_of(CHUNK)
    gain = gain_ref[...]
    for seq in range(seqs):
        _, _, _, forget, queries, keys, values = gates_of(proj_ref[0, seq], bound_ref[...], width)
        total = split_sum(tri, jnp.log(forget))
        middle = total[mid : mid + 1]
        end = total[CHUNK - 1 : CHUNK]
        query_near = queries * jnp.exp(total - middle)
        key_near = keys * jnp.exp(middle - total)
        query_far = (query_near * jnp.exp(middle)).astype(BF)
        key_far = (key_near * jnp.exp(end - middle)).astype(BF)
        query_near = query_near.astype(BF)
        key_near = key_near.astype(BF)
        decay = jnp.exp(end)
        for head in range(heads):
            cut = slice(head * hd, (head + 1) * hd)
            at = seq * heads + head
            state = state_ref[at]
            state_low = state.astype(BF)
            states_ref[0, at] = state_low
            scores = mm(query_near[:, cut], key_near[:, cut], 1, 1)
            scores = jnp.where(causal, scores, 0.0).astype(BF)
            mixed = mm(query_far[:, cut], state_low, 1, 1) + mm(scores, values[:, cut], 1, 0)
            state_ref[at] = state * decay[:, cut] + mm(values[:, cut], key_far[:, cut], 0, 0)
            scale = lax.rsqrt(jnp.mean(mixed * mixed, axis=-1, keepdims=True) + EPS)
            mixed_ref[0, seq, :, cut] = mixed
            head_ref[0, seq, :, cut] = (mixed * scale * gain).astype(BF)


def backward_body(
    own_ref,
    proj_ref,
    mixed_ref,
    out_ref,
    states_ref,
    bound_ref,
    gain_ref,
    grad_ref,
    bound_sum_ref,
    head_sum_ref,
    back_ref,
):
    seqs = proj_ref.shape[1]
    width = proj_ref.shape[3] // 3
    hd = gain_ref.shape[1]
    heads = width // hd
    mid = CHUNK // 2 - 1

    @pl.when(pl.program_id(0) == 0)
    def _():
        back_ref[...] = jnp.zeros_like(back_ref)
        bound_sum_ref[...] = jnp.zeros_like(bound_sum_ref)
        head_sum_ref[...] = jnp.zeros_like(head_sum_ref)

    tri = order_masks(CHUNK, lambda row, col: col <= row)
    tri_up = order_masks(CHUNK, lambda row, col: col >= row)
    tri_under = order_masks(CHUNK, lambda row, col: col < row)
    causal = causal_of(CHUNK)
    gain = gain_ref[...]
    bound = bound_ref[...]
    head_sum = jnp.zeros((1, hd), F32)
    bound_sum = jnp.zeros((1, width), F32)
    for seq in range(seqs):
        query_pre, sig_query, sig_forget, forget, queries, keys, values = gates_of(
            proj_ref[0, seq], bound, width
        )
        total = split_sum(tri, jnp.log(forget))
        middle = total[mid : mid + 1]
        end = total[CHUNK - 1 : CHUNK]
        exp_query = jnp.exp(total - middle)
        exp_key = jnp.exp(middle - total)
        query_near_f = queries * exp_query
        key_near_f = keys * exp_key
        exp_mid = jnp.exp(middle)
        exp_rest = jnp.exp(end - middle)
        query_far = (query_near_f * exp_mid).astype(BF)
        key_far = (key_near_f * exp_rest).astype(BF)
        query_near = query_near_f.astype(BF)
        key_near = key_near_f.astype(BF)
        decay = jnp.exp(end)
        later_parts = []
        sooner_parts = []
        edge_parts = []
        query_parts = []
        key_parts = []
        value_parts = []
        for head in range(heads):
            cut = slice(head * hd, (head + 1) * hd)
            at = seq * heads + head
            mixed = mixed_ref[0, seq, :, cut]
            out_head = out_ref[0, seq, :, cut].astype(F32)
            scale = lax.rsqrt(jnp.mean(mixed * mixed, axis=-1, keepdims=True) + EPS)
            weighted = gain * out_head
            along = jnp.mean(weighted * mixed, axis=-1, keepdims=True)
            grad = (scale * weighted - mixed * ((scale * scale * scale) * along)).astype(BF)
            head_sum = head_sum + jnp.sum(out_head * mixed * scale, axis=0, keepdims=True)
            state_low = states_ref[0, at]
            back = back_ref[at]
            back_low = back.astype(BF)
            value = values[:, cut]
            scores = mm(query_near[:, cut], key_near[:, cut], 1, 1)
            scores = jnp.where(causal, scores, 0.0).astype(BF)
            cross = mm(grad, value, 1, 1)
            cross = jnp.where(causal, cross, 0.0).astype(BF)
            query_far_grad = exp_mid[:, cut] * mm(grad, state_low, 1, 0)
            query_near_grad = mm(cross, key_near[:, cut], 1, 0)
            key_far_grad = exp_rest[:, cut] * mm(value, back_low, 1, 0)
            key_near_grad = mm(cross, query_near[:, cut], 0, 0)
            query_low = query_near[:, cut].astype(F32)
            key_low = key_near[:, cut].astype(F32)
            later_parts.append(query_low * (query_far_grad + query_near_grad) - key_low * key_near_grad)
            sooner_parts.append(key_low * key_far_grad)
            edge_parts.append(
                decay[:, cut] * jnp.sum(state_low.astype(F32) * back, axis=0, keepdims=True)
            )
            query_parts.append(exp_query[:, cut] * (query_far_grad + query_near_grad))
            key_parts.append(exp_key[:, cut] * (key_far_grad + key_near_grad))
            value_parts.append(mm(key_far[:, cut], back_low, 1, 1) + mm(scores, grad, 0, 0))
            back_ref[at] = back * decay[:, cut] + mm(grad, query_far[:, cut], 0, 0)
        query_grad = jnp.concatenate(query_parts, axis=1)
        key_grad = jnp.concatenate(key_parts, axis=1)
        log_grad = (
            split_sum(tri_up, jnp.concatenate(later_parts, axis=1))
            + split_sum(tri_under, jnp.concatenate(sooner_parts, axis=1))
            + jnp.concatenate(edge_parts, axis=1)
        )
        forget_grad = log_grad / forget - key_grad
        bound_sum = bound_sum + jnp.sum(forget_grad * (1.0 - sig_forget), axis=0, keepdims=True)
        grad_ref[0, seq, :, :width] = (
            query_grad * sig_query * (1.0 + query_pre * (1.0 - sig_query))
        ).astype(BF)
        grad_ref[0, seq, :, width : 2 * width] = (
            forget_grad * (1.0 - bound) * sig_forget * (1.0 - sig_forget)
        ).astype(BF)
        grad_ref[0, seq, :, 2 * width :] = jnp.concatenate(value_parts, axis=1).astype(BF)
    bound_sum_ref[...] += bound_sum
    head_sum_ref[...] += head_sum


def place_of(chunk, own, per_piece):
    return lax.bitwise_xor(chunk // per_piece, own), chunk % per_piece


def recur_forward(own, proj, bound, gain):
    pieces, seqs, rows, three = proj.shape
    width = three // 3
    hd = gain.shape[1]
    per = rows // CHUNK
    chunks = pieces * per
    many = seqs * width // hd

    def rows_at(chunk, own_ref):
        piece, block = place_of(chunk, own_ref[0], per)
        return (piece, 0, block, 0)

    return pl.pallas_call(
        forward_body,
        grid_spec=pltpu.PrefetchScalarGridSpec(
            num_scalar_prefetch=1,
            grid=(chunks,),
            in_specs=[
                pl.BlockSpec((1, seqs, CHUNK, three), rows_at),
                pl.BlockSpec((1, width), lambda chunk, own_ref: (0, 0)),
                pl.BlockSpec((1, hd), lambda chunk, own_ref: (0, 0)),
            ],
            out_specs=[
                pl.BlockSpec((1, seqs, CHUNK, width), rows_at),
                pl.BlockSpec((1, seqs, CHUNK, width), rows_at),
                pl.BlockSpec((1, many, hd, hd), lambda chunk, own_ref: (chunk, 0, 0, 0)),
            ],
            scratch_shapes=[pltpu.VMEM((many, hd, hd), F32)],
        ),
        out_shape=[
            jax.ShapeDtypeStruct((pieces, seqs, rows, width), F32),
            jax.ShapeDtypeStruct((pieces, seqs, rows, width), BF),
            jax.ShapeDtypeStruct((chunks, many, hd, hd), BF),
        ],
        compiler_params=pltpu.CompilerParams(
            dimension_semantics=("arbitrary",), vmem_limit_bytes=32 * 1024 * 1024
        ),
        cost_estimate=pl.CostEstimate(flops=1, bytes_accessed=1, transcendentals=0),
        name="recur_forward",
    )(own, proj, bound, gain)


def recur_backward(own, proj, mixed, out_head, states, bound, gain):
    pieces, seqs, rows, three = proj.shape
    width = three // 3
    hd = gain.shape[1]
    per = rows // CHUNK
    chunks = pieces * per
    many = seqs * width // hd

    def rows_at(step, own_ref):
        piece, block = place_of(chunks - 1 - step, own_ref[0], per)
        return (piece, 0, block, 0)

    return pl.pallas_call(
        backward_body,
        grid_spec=pltpu.PrefetchScalarGridSpec(
            num_scalar_prefetch=1,
            grid=(chunks,),
            in_specs=[
                pl.BlockSpec((1, seqs, CHUNK, three), rows_at),
                pl.BlockSpec((1, seqs, CHUNK, width), rows_at),
                pl.BlockSpec((1, seqs, CHUNK, width), rows_at),
                pl.BlockSpec((1, many, hd, hd), lambda step, own_ref: (chunks - 1 - step, 0, 0, 0)),
                pl.BlockSpec((1, width), lambda step, own_ref: (0, 0)),
                pl.BlockSpec((1, hd), lambda step, own_ref: (0, 0)),
            ],
            out_specs=[
                pl.BlockSpec((1, seqs, CHUNK, three), rows_at),
                pl.BlockSpec((1, width), lambda step, own_ref: (0, 0)),
                pl.BlockSpec((1, hd), lambda step, own_ref: (0, 0)),
            ],
            scratch_shapes=[pltpu.VMEM((many, hd, hd), F32)],
        ),
        out_shape=[
            jax.ShapeDtypeStruct((pieces, seqs, rows, three), BF),
            jax.ShapeDtypeStruct((1, width), F32),
            jax.ShapeDtypeStruct((1, hd), F32),
        ],
        compiler_params=pltpu.CompilerParams(
            dimension_semantics=("arbitrary",), vmem_limit_bytes=32 * 1024 * 1024
        ),
        cost_estimate=pl.CostEstimate(flops=1, bytes_accessed=1, transcendentals=0),
        name="recur_backward",
    )(own, proj, mixed, out_head, states, bound, gain)


def rms_rows(values, gain_vec):
    scaling = lax.rsqrt(jnp.mean(values * values, axis=-1, keepdims=True) + EPS)
    return values * scaling * gain_vec, scaling


def norm_back(values, scaling, gain_vec, upstream):
    weighted = gain_vec * upstream
    along = jnp.mean(weighted * values, axis=-1, keepdims=True)
    return (
        scaling * weighted - values * (scaling * scaling * scaling) * along,
        upstream * values * scaling,
    )


AXES = ("dp", "tensor")


def make_local(dp_size, tensor_size):
    columns = dp_size // 2
    groups = [[2 * col + core for col in range(columns)] for core in range(2)]

    def route(step, invert=False):
        pairs = []
        for dp in range(dp_size):
            for z in range(tensor_size):
                col, core, place = step(dp >> 1, dp & 1, z)
                pair = (dp * tensor_size + z, (col * 2 + core) * tensor_size + place)
                pairs.append(pair[::-1] if invert else pair)
        return sorted(pairs)

    def spread(flip):
        return lambda col, core, z: (col, z & 1, 2 * (core ^ flip) + (z >> 1))

    spreads = [route(spread(flip)) for flip in (0, 1)]
    returns = [route(spread(flip), True) for flip in (0, 1)]
    core_swap = route(lambda col, core, z: (col, core ^ 1, z))
    z_swap = route(lambda col, core, z: (col, core, z ^ 1))

    def move(array, pairs):
        return lax.ppermute(array, AXES, pairs)

    def sum_steps(array, steps):
        total = dp_size * tensor_size
        for step in steps:
            array = array + move(array, [(at, at ^ (1 << step)) for at in range(total)])
        return array

    low_steps = range(tensor_size.bit_length() - 1)
    high_steps = range(tensor_size.bit_length() - 1, (dp_size * tensor_size).bit_length() - 1)

    def after(array, *earlier):
        return lax.optimization_barrier((array, *earlier))[0]

    def ordered(first, second, swap):
        return jnp.where(swap, second, first), jnp.where(swap, first, second)

    def spread_weight(shard):
        return move(shard, spreads[0]), move(shard, spreads[1])

    def joined(pair, swap):
        return jnp.concatenate(ordered(*pair, swap), axis=0)

    def gather_weight(pair):
        return lax.all_gather(pair, "dp", axis=0, tiled=True, axis_index_groups=groups)

    def scatter_grad(whole):
        return lax.psum_scatter(
            whole, "dp", scatter_dimension=0, tiled=True, axis_index_groups=groups
        )

    def return_grad(pair, swap, *earlier):
        rows = pair.shape[0] // 2
        first, second = ordered(pair[:rows], pair[rows:], swap)
        first = move(after(first, *earlier), returns[0])
        return first, move(after(second, first), returns[1])

    def whole_grad(parts):
        return parts[0].astype(F32) + parts[1].astype(F32)

    def gather_rows(own):
        near = move(own, core_swap)
        far = move(own, z_swap)
        return jnp.stack([own, near, far, move(far, core_swap)])

    def scatter_far(far_pair):
        return (far_pair[0].astype(F32) + move(far_pair[1], core_swap).astype(F32)).astype(BF)

    def scatter_own(arrived, own_pair):
        near = own_pair[0].astype(F32) + move(own_pair[1], core_swap).astype(F32)
        return near + arrived.astype(F32)

    def scatter_rows(far_pair, own_pair):
        return scatter_own(move(scatter_far(far_pair), z_swap), own_pair)

    def split_rows(compute, *arrays):
        half = arrays[0].shape[0] // 2
        return [compute(*(array[at:to] for array in arrays)) for at, to in ((half, 2 * half), (0, half))]

    def dot_rows(first_mat, second_mat, second_dim):
        return lax.dot_general(
            first_mat,
            second_mat,
            (((first_mat.ndim - 1,), (second_dim,)), ((), ())),
            preferred_element_type=F32,
        )

    def local(
        tokens,
        lengths,
        norm_gain,
        mixer_in,
        lower_bound,
        head_gain,
        head_merge,
        feed_gain,
        gate_up,
        down_weight,
        out_grad,
    ):
        seqs, rows, model = tokens.shape
        dp_at = lax.axis_index("dp")
        z_at = lax.axis_index("tensor")
        half_at = z_at // 2
        role = 2 * (z_at % 2) + dp_at % 2

        def weight_grad(first_mat, second_mat):
            return lax.dot_general(
                first_mat.reshape(-1, first_mat.shape[-1]),
                second_mat.reshape(-1, second_mat.shape[-1]),
                (((0,), (0,)), ((), ())),
                preferred_element_type=F32,
            ).astype(BF)

        swap = half_at == 1
        lens = move(lengths, spreads[0])
        mixer_pair = spread_weight(mixer_in.reshape(mixer_in.shape[0], -1))
        vectors = [norm_gain, feed_gain, head_gain, lower_bound]
        vector_ends = np.cumsum([vector.shape[0] for vector in vectors])
        packed = jnp.zeros((dp_size, vector_ends[-1]), BF)
        packed = lax.dynamic_update_slice_in_dim(packed, jnp.concatenate(vectors)[None], dp_at, 0)
        packed = sum_steps(packed, high_steps)
        tok = move(after(tokens, packed), spreads[0])
        merge_pair = spread_weight(after(head_merge, tok))

        bounds = jnp.zeros((tensor_size, dp_size, lower_bound.shape[0]), BF)
        bounds = lax.dynamic_update_slice_in_dim(bounds, packed[None, :, vector_ends[2] :], z_at, 0)
        bounds = sum_steps(bounds, low_steps)
        vector_rows = packed.astype(F32)
        norm_vec = vector_rows[:, : vector_ends[0]].reshape(-1)
        feed_vec = vector_rows[:, vector_ends[0] : vector_ends[1]].reshape(-1)
        head_vec = vector_rows[:, vector_ends[1] : vector_ends[2]].reshape(1, -1)
        bound_vec = lax.dynamic_index_in_dim(bounds, role, 0, False).astype(F32).reshape(1, -1)

        positions = role * rows + jnp.arange(rows, dtype=jnp.int32)
        valid = (positions[None, :] < lens[:, None]).astype(F32)[:, :, None]
        own = role.astype(jnp.int32).reshape(1)

        masked = tok.astype(F32) * valid
        normed, scale_one = rms_rows(masked, norm_vec)
        normed = normed.astype(BF)
        gates_pair = spread_weight(after(gate_up.reshape(gate_up.shape[0], -1), normed, *merge_pair))
        down_pair = spread_weight(after(down_weight, *gates_pair))
        out_rows = move(after(out_grad, *down_pair), spreads[0])
        mixer_mat = gather_weight(joined(mixer_pair, swap))
        merge_mat = gather_weight(joined(merge_pair, swap))
        first_in = gather_rows(normed)
        gates_mat = gather_weight(joined([after(part, first_in) for part in gates_pair], swap))
        down_mat = gather_weight(joined(down_pair, swap))
        projected = dot_rows(first_in, mixer_mat, 0)
        mixed, head_out, states = recur_forward(own, projected, bound_vec, head_vec)
        attn = scatter_rows(*split_rows(lambda part: dot_rows(part, merge_mat, 0).astype(BF), head_out))
        middle = masked + attn
        normed_two, scale_two = rms_rows(middle, feed_vec)
        upstream = out_rows.astype(F32) * valid
        branch_in = gather_rows(upstream.astype(BF))
        second_in = after(gather_rows(normed_two.astype(BF)), branch_in)
        gate_pre = dot_rows(second_in, gates_mat, 0)
        hidden_cols = down_mat.shape[0]
        gate_part = gate_pre[..., :hidden_cols]
        up_part = gate_pre[..., hidden_cols:]
        sig_gate = jax.nn.sigmoid(gate_part)
        hidden = (gate_part * sig_gate * up_part).astype(BF)
        down_whole = weight_grad(hidden, branch_in)
        down_pair = scatter_grad(after(down_whole, down_mat))
        down_grad = return_grad(down_pair, swap)
        hidden_grad = dot_rows(after(branch_in, down_whole), down_mat, 1)
        gate_grad = hidden_grad * up_part * sig_gate * (1.0 + gate_part * (1.0 - sig_gate))
        up_grad = hidden_grad * gate_part * sig_gate
        both_grad = jnp.concatenate([gate_grad, up_grad], axis=-1).astype(BF)
        second_parts = split_rows(lambda part: dot_rows(part, gates_mat, 1).astype(BF), both_grad)
        second_far = scatter_far(second_parts[0])
        gates_whole = weight_grad(second_in, after(both_grad, second_far, *second_parts))
        second_far = move(second_far, z_swap)
        gates_pair = scatter_grad(after(gates_whole, down_pair, second_far))
        second_grad = after(scatter_own(second_far, second_parts[1]), gates_whole)
        middle_grad, feed_terms = norm_back(middle, scale_two, feed_vec, second_grad)
        middle_grad = middle_grad + upstream
        feed_parts = split_rows(lambda part: dot_rows(part, down_mat, 0).astype(BF), hidden)
        attn_in = after(gather_rows(middle_grad.astype(BF)), *feed_parts)
        feed_far = move(after(scatter_far(feed_parts[0]), attn_in), z_swap)
        feed_out = scatter_own(feed_far, feed_parts[1])
        block_out = move(after((valid * (middle + feed_out)).astype(BF), *down_grad), returns[0])
        out_head = dot_rows(attn_in, merge_mat, 1)
        proj_grad, bound_sum, head_sum = recur_backward(
            own, projected, mixed, out_head, states, bound_vec, head_vec
        )
        first_parts = split_rows(lambda part: dot_rows(part, mixer_mat, 1).astype(BF), proj_grad)
        first_far = move(scatter_far(first_parts[0]), z_swap)
        first_grad = scatter_own(first_far, first_parts[1])
        merge_whole = weight_grad(head_out, attn_in)
        mixer_whole = weight_grad(first_in, proj_grad)
        mixer_pair = scatter_grad(after(mixer_whole, gates_pair, *first_parts, *down_grad, block_out))
        gates_grad = return_grad(gates_pair, swap, block_out)
        first_grad = after(first_grad, merge_whole, mixer_whole, gates_grad[0])
        masked_grad, norm_terms = norm_back(masked, scale_one, norm_vec, first_grad)
        input_rows = (valid * (masked_grad + middle_grad)).astype(BF)

        merge_pair = scatter_grad(after(merge_whole, mixer_pair, gates_grad[1]))
        input_grad = move(after(input_rows, *gates_grad), returns[0])
        mixer_grad = return_grad(mixer_pair, swap, input_grad)
        merge_grad = return_grad(merge_pair, swap, *mixer_grad)

        bound_all = jnp.zeros((tensor_size, bound_sum.shape[1]), F32)
        bound_all = lax.dynamic_update_slice_in_dim(bound_all, bound_sum, role, 0)
        sums = [
            jnp.sum(norm_terms, axis=(0, 1)),
            jnp.sum(feed_terms, axis=(0, 1)),
            head_sum.reshape(-1),
            bound_all.reshape(-1),
        ]
        ends = np.cumsum([part.shape[0] for part in sums])
        summed = sum_steps(jnp.concatenate(sums), [*low_steps, *high_steps])

        def shard_of(vector, count, at):
            return lax.dynamic_slice_in_dim(vector, at * count, count, 0)

        return (
            block_out,
            input_grad,
            shard_of(summed[: ends[0]], norm_gain.shape[0], dp_at),
            whole_grad(mixer_grad).reshape(mixer_in.shape),
            shard_of(summed[ends[2] :], lower_bound.shape[0], z_at * dp_size + dp_at),
            shard_of(summed[ends[1] : ends[2]], head_gain.shape[0], dp_at),
            whole_grad(merge_grad),
            shard_of(summed[ends[0] : ends[1]], feed_gain.shape[0], dp_at),
            whole_grad(gates_grad).reshape(gate_up.shape),
            whole_grad(down_grad),
        )

    return local


def solution(mesh):
    rows_spec = P("dp", "tensor", None)
    wide_spec = P("dp", None, "tensor")
    tall_spec = P(("tensor", "dp"), None)
    return jax.shard_map(
        make_local(mesh.shape["dp"], mesh.shape["tensor"]),
        mesh=mesh,
        in_specs=(
            rows_spec,
            P("dp"),
            P("dp"),
            wide_spec,
            P(("tensor", "dp")),
            P("dp"),
            tall_spec,
            P("dp"),
            wide_spec,
            tall_spec,
            rows_spec,
        ),
        out_specs=(
            rows_spec,
            rows_spec,
            P("dp"),
            wide_spec,
            P(("tensor", "dp")),
            P("dp"),
            tall_spec,
            P("dp"),
            wide_spec,
            tall_spec,
        ),
        check_vma=False,
    )
```

```python
import functools

import jax
import jax.numpy as jnp
import numpy as np
from jax import lax
from jax.experimental import pallas as pl
from jax.experimental.pallas import tpu as pltpu
from jax.sharding import PartitionSpec as P

EPS = 1e-06
CHUNK = 32
BF = jnp.bfloat16
F32 = jnp.float32


def mm(first_mat, second_mat, first_dim, second_dim):
    return lax.dot_general(
        first_mat, second_mat, (((first_dim,), (second_dim,)), ((), ())), preferred_element_type=F32
    )


def split_sum(mask_two, values):
    high = values.astype(BF)
    rest = (values - high.astype(F32)).astype(BF)
    return mm(mask_two, jnp.concatenate([high, rest], axis=0), 1, 0)


def order_masks(size, keep):
    row = lax.broadcasted_iota(jnp.int32, (size, 2 * size), 0)
    col = lax.broadcasted_iota(jnp.int32, (size, 2 * size), 1)
    col = jnp.where(col >= size, col - size, col)
    return keep(row, col).astype(F32).astype(BF)


def causal_of(size):
    row = lax.broadcasted_iota(jnp.int32, (size, size), 0)
    col = lax.broadcasted_iota(jnp.int32, (size, size), 1)
    return col <= row


def gates_of(proj, bound, width):
    query_pre = proj[:, :width]
    sig_query = jax.nn.sigmoid(query_pre)
    sig_forget = jax.nn.sigmoid(proj[:, width : 2 * width])
    forget = bound + (1.0 - bound) * sig_forget
    queries = (query_pre * sig_query).astype(BF).astype(F32)
    keys = (1.0 - forget).astype(BF).astype(F32)
    values = proj[:, 2 * width :].astype(BF)
    return query_pre, sig_query, sig_forget, forget, queries, keys, values


def forward_body(own_ref, proj_ref, bound_ref, gain_ref, mixed_ref, head_ref, states_ref, state_ref):
    seqs = proj_ref.shape[1]
    width = proj_ref.shape[3] // 3
    hd = gain_ref.shape[1]
    heads = width // hd
    mid = CHUNK // 2 - 1

    @pl.when(pl.program_id(0) == 0)
    def _():
        state_ref[...] = jnp.zeros_like(state_ref)

    tri = order_masks(CHUNK, lambda row, col: col <= row)
    causal = causal_of(CHUNK)
    gain = gain_ref[...]
    for seq in range(seqs):
        _, _, _, forget, queries, keys, values = gates_of(proj_ref[0, seq], bound_ref[...], width)
        total = split_sum(tri, jnp.log(forget))
        middle = total[mid : mid + 1]
        end = total[CHUNK - 1 : CHUNK]
        query_near = queries * jnp.exp(total - middle)
        key_near = keys * jnp.exp(middle - total)
        query_far = (query_near * jnp.exp(middle)).astype(BF)
        key_far = (key_near * jnp.exp(end - middle)).astype(BF)
        query_near = query_near.astype(BF)
        key_near = key_near.astype(BF)
        decay = jnp.exp(end)
        for head in range(heads):
            cut = slice(head * hd, (head + 1) * hd)
            at = seq * heads + head
            state = state_ref[at]
            state_low = state.astype(BF)
            states_ref[0, at] = state_low
            scores = mm(query_near[:, cut], key_near[:, cut], 1, 1)
            scores = jnp.where(causal, scores, 0.0).astype(BF)
            mixed = mm(query_far[:, cut], state_low, 1, 1) + mm(scores, values[:, cut], 1, 0)
            state_ref[at] = state * decay[:, cut] + mm(values[:, cut], key_far[:, cut], 0, 0)
            scale = lax.rsqrt(jnp.mean(mixed * mixed, axis=-1, keepdims=True) + EPS)
            mixed_ref[0, seq, :, cut] = mixed
            head_ref[0, seq, :, cut] = (mixed * scale * gain).astype(BF)


def backward_body(
    own_ref,
    proj_ref,
    mixed_ref,
    out_ref,
    states_ref,
    bound_ref,
    gain_ref,
    grad_ref,
    bound_sum_ref,
    head_sum_ref,
    back_ref,
):
    seqs = proj_ref.shape[1]
    width = proj_ref.shape[3] // 3
    hd = gain_ref.shape[1]
    heads = width // hd
    mid = CHUNK // 2 - 1

    @pl.when(pl.program_id(0) == 0)
    def _():
        back_ref[...] = jnp.zeros_like(back_ref)
        bound_sum_ref[...] = jnp.zeros_like(bound_sum_ref)
        head_sum_ref[...] = jnp.zeros_like(head_sum_ref)

    tri = order_masks(CHUNK, lambda row, col: col <= row)
    tri_up = order_masks(CHUNK, lambda row, col: col >= row)
    tri_under = order_masks(CHUNK, lambda row, col: col < row)
    causal = causal_of(CHUNK)
    gain = gain_ref[...]
    bound = bound_ref[...]
    head_sum = jnp.zeros((1, hd), F32)
    bound_sum = jnp.zeros((1, width), F32)
    for seq in range(seqs):
        query_pre, sig_query, sig_forget, forget, queries, keys, values = gates_of(
            proj_ref[0, seq], bound, width
        )
        total = split_sum(tri, jnp.log(forget))
        middle = total[mid : mid + 1]
        end = total[CHUNK - 1 : CHUNK]
        exp_query = jnp.exp(total - middle)
        exp_key = jnp.exp(middle - total)
        query_near_f = queries * exp_query
        key_near_f = keys * exp_key
        exp_mid = jnp.exp(middle)
        exp_rest = jnp.exp(end - middle)
        query_far = (query_near_f * exp_mid).astype(BF)
        key_far = (key_near_f * exp_rest).astype(BF)
        query_near = query_near_f.astype(BF)
        key_near = key_near_f.astype(BF)
        decay = jnp.exp(end)
        later_parts = []
        sooner_parts = []
        edge_parts = []
        query_parts = []
        key_parts = []
        value_parts = []
        for head in range(heads):
            cut = slice(head * hd, (head + 1) * hd)
            at = seq * heads + head
            mixed = mixed_ref[0, seq, :, cut]
            out_head = out_ref[0, seq, :, cut].astype(F32)
            scale = lax.rsqrt(jnp.mean(mixed * mixed, axis=-1, keepdims=True) + EPS)
            weighted = gain * out_head
            along = jnp.mean(weighted * mixed, axis=-1, keepdims=True)
            grad = (scale * weighted - mixed * ((scale * scale * scale) * along)).astype(BF)
            head_sum = head_sum + jnp.sum(out_head * mixed * scale, axis=0, keepdims=True)
            state_low = states_ref[0, at]
            back = back_ref[at]
            back_low = back.astype(BF)
            value = values[:, cut]
            scores = mm(query_near[:, cut], key_near[:, cut], 1, 1)
            scores = jnp.where(causal, scores, 0.0).astype(BF)
            cross = mm(grad, value, 1, 1)
            cross = jnp.where(causal, cross, 0.0).astype(BF)
            query_far_grad = exp_mid[:, cut] * mm(grad, state_low, 1, 0)
            query_near_grad = mm(cross, key_near[:, cut], 1, 0)
            key_far_grad = exp_rest[:, cut] * mm(value, back_low, 1, 0)
            key_near_grad = mm(cross, query_near[:, cut], 0, 0)
            query_low = query_near[:, cut].astype(F32)
            key_low = key_near[:, cut].astype(F32)
            later_parts.append(query_low * (query_far_grad + query_near_grad) - key_low * key_near_grad)
            sooner_parts.append(key_low * key_far_grad)
            edge_parts.append(
                decay[:, cut] * jnp.sum(state_low.astype(F32) * back, axis=0, keepdims=True)
            )
            query_parts.append(exp_query[:, cut] * (query_far_grad + query_near_grad))
            key_parts.append(exp_key[:, cut] * (key_far_grad + key_near_grad))
            value_parts.append(mm(key_far[:, cut], back_low, 1, 1) + mm(scores, grad, 0, 0))
            back_ref[at] = back * decay[:, cut] + mm(grad, query_far[:, cut], 0, 0)
        query_grad = jnp.concatenate(query_parts, axis=1)
        key_grad = jnp.concatenate(key_parts, axis=1)
        log_grad = (
            split_sum(tri_up, jnp.concatenate(later_parts, axis=1))
            + split_sum(tri_under, jnp.concatenate(sooner_parts, axis=1))
            + jnp.concatenate(edge_parts, axis=1)
        )
        forget_grad = log_grad / forget - key_grad
        bound_sum = bound_sum + jnp.sum(forget_grad * (1.0 - sig_forget), axis=0, keepdims=True)
        grad_ref[0, seq, :, :width] = (
            query_grad * sig_query * (1.0 + query_pre * (1.0 - sig_query))
        ).astype(BF)
        grad_ref[0, seq, :, width : 2 * width] = (
            forget_grad * (1.0 - bound) * sig_forget * (1.0 - sig_forget)
        ).astype(BF)
        grad_ref[0, seq, :, 2 * width :] = jnp.concatenate(value_parts, axis=1).astype(BF)
    bound_sum_ref[...] += bound_sum
    head_sum_ref[...] += head_sum


def place_of(chunk, own, per_piece):
    return lax.bitwise_xor(chunk // per_piece, own), chunk % per_piece


def recur_forward(own, proj, bound, gain):
    pieces, seqs, rows, three = proj.shape
    width = three // 3
    hd = gain.shape[1]
    per = rows // CHUNK
    chunks = pieces * per
    many = seqs * width // hd

    def rows_at(chunk, own_ref):
        piece, block = place_of(chunk, own_ref[0], per)
        return (piece, 0, block, 0)

    return pl.pallas_call(
        forward_body,
        grid_spec=pltpu.PrefetchScalarGridSpec(
            num_scalar_prefetch=1,
            grid=(chunks,),
            in_specs=[
                pl.BlockSpec((1, seqs, CHUNK, three), rows_at),
                pl.BlockSpec((1, width), lambda chunk, own_ref: (0, 0)),
                pl.BlockSpec((1, hd), lambda chunk, own_ref: (0, 0)),
            ],
            out_specs=[
                pl.BlockSpec((1, seqs, CHUNK, width), rows_at),
                pl.BlockSpec((1, seqs, CHUNK, width), rows_at),
                pl.BlockSpec((1, many, hd, hd), lambda chunk, own_ref: (chunk, 0, 0, 0)),
            ],
            scratch_shapes=[pltpu.VMEM((many, hd, hd), F32)],
        ),
        out_shape=[
            jax.ShapeDtypeStruct((pieces, seqs, rows, width), F32),
            jax.ShapeDtypeStruct((pieces, seqs, rows, width), BF),
            jax.ShapeDtypeStruct((chunks, many, hd, hd), BF),
        ],
        compiler_params=pltpu.CompilerParams(
            dimension_semantics=("arbitrary",), vmem_limit_bytes=32 * 1024 * 1024
        ),
        cost_estimate=pl.CostEstimate(flops=1, bytes_accessed=1, transcendentals=0),
        name="recur_forward",
    )(own, proj, bound, gain)


def recur_backward(own, proj, mixed, out_head, states, bound, gain):
    pieces, seqs, rows, three = proj.shape
    width = three // 3
    hd = gain.shape[1]
    per = rows // CHUNK
    chunks = pieces * per
    many = seqs * width // hd

    def rows_at(step, own_ref):
        piece, block = place_of(chunks - 1 - step, own_ref[0], per)
        return (piece, 0, block, 0)

    return pl.pallas_call(
        backward_body,
        grid_spec=pltpu.PrefetchScalarGridSpec(
            num_scalar_prefetch=1,
            grid=(chunks,),
            in_specs=[
                pl.BlockSpec((1, seqs, CHUNK, three), rows_at),
                pl.BlockSpec((1, seqs, CHUNK, width), rows_at),
                pl.BlockSpec((1, seqs, CHUNK, width), rows_at),
                pl.BlockSpec((1, many, hd, hd), lambda step, own_ref: (chunks - 1 - step, 0, 0, 0)),
                pl.BlockSpec((1, width), lambda step, own_ref: (0, 0)),
                pl.BlockSpec((1, hd), lambda step, own_ref: (0, 0)),
            ],
            out_specs=[
                pl.BlockSpec((1, seqs, CHUNK, three), rows_at),
                pl.BlockSpec((1, width), lambda step, own_ref: (0, 0)),
                pl.BlockSpec((1, hd), lambda step, own_ref: (0, 0)),
            ],
            scratch_shapes=[pltpu.VMEM((many, hd, hd), F32)],
        ),
        out_shape=[
            jax.ShapeDtypeStruct((pieces, seqs, rows, three), BF),
            jax.ShapeDtypeStruct((1, width), F32),
            jax.ShapeDtypeStruct((1, hd), F32),
        ],
        compiler_params=pltpu.CompilerParams(
            dimension_semantics=("arbitrary",), vmem_limit_bytes=32 * 1024 * 1024
        ),
        cost_estimate=pl.CostEstimate(flops=1, bytes_accessed=1, transcendentals=0),
        name="recur_backward",
    )(own, proj, mixed, out_head, states, bound, gain)


def rms_rows(values, gain_vec):
    scaling = lax.rsqrt(jnp.mean(values * values, axis=-1, keepdims=True) + EPS)
    return values * scaling * gain_vec, scaling


def norm_back(values, scaling, gain_vec, upstream):
    weighted = gain_vec * upstream
    along = jnp.mean(weighted * values, axis=-1, keepdims=True)
    return (
        scaling * weighted - values * (scaling * scaling * scaling) * along,
        upstream * values * scaling,
    )


AXES = ("dp", "tensor")


def make_local(dp_size, tensor_size):
    columns = dp_size // 2
    groups = [[2 * col + core for col in range(columns)] for core in range(2)]

    def route(step, invert=False):
        pairs = []
        for dp in range(dp_size):
            for z in range(tensor_size):
                col, core, place = step(dp >> 1, dp & 1, z)
                pair = (dp * tensor_size + z, (col * 2 + core) * tensor_size + place)
                pairs.append(pair[::-1] if invert else pair)
        return sorted(pairs)

    def spread(flip):
        return lambda col, core, z: (col, z & 1, 2 * (core ^ flip) + (z >> 1))

    spreads = [route(spread(flip)) for flip in (0, 1)]
    returns = [route(spread(flip), True) for flip in (0, 1)]
    core_swap = route(lambda col, core, z: (col, core ^ 1, z))
    z_swap = route(lambda col, core, z: (col, core, z ^ 1))

    def move(array, pairs):
        return lax.ppermute(array, AXES, pairs)

    def sum_steps(array, steps):
        total = dp_size * tensor_size
        for step in steps:
            array = array + move(array, [(at, at ^ (1 << step)) for at in range(total)])
        return array

    low_steps = range(tensor_size.bit_length() - 1)
    high_steps = range(tensor_size.bit_length() - 1, (dp_size * tensor_size).bit_length() - 1)

    def after(array, *earlier):
        return lax.optimization_barrier((array, *earlier))[0]

    def ordered(first, second, swap):
        return jnp.where(swap, second, first), jnp.where(swap, first, second)

    def spread_weight(shard):
        return move(shard, spreads[0]), move(shard, spreads[1])

    def joined(pair, swap):
        return jnp.concatenate(ordered(*pair, swap), axis=0)

    def gather_weight(pair):
        return lax.all_gather(pair, "dp", axis=0, tiled=True, axis_index_groups=groups)

    def scatter_grad(whole):
        return lax.psum_scatter(
            whole, "dp", scatter_dimension=0, tiled=True, axis_index_groups=groups
        )

    def return_grad(pair, swap, *earlier):
        rows = pair.shape[0] // 2
        first, second = ordered(pair[:rows], pair[rows:], swap)
        first = move(after(first, *earlier), returns[0])
        return first, move(after(second, first), returns[1])

    def whole_grad(parts):
        return parts[0].astype(F32) + parts[1].astype(F32)

    def gather_rows(own):
        near = move(own, core_swap)
        far = move(own, z_swap)
        return jnp.stack([own, near, far, move(far, core_swap)])

    def scatter_far(far_pair):
        return (far_pair[0].astype(F32) + move(far_pair[1], core_swap).astype(F32)).astype(BF)

    def scatter_own(arrived, own_pair):
        near = own_pair[0].astype(F32) + move(own_pair[1], core_swap).astype(F32)
        return near + arrived.astype(F32)

    def scatter_rows(far_pair, own_pair):
        return scatter_own(move(scatter_far(far_pair), z_swap), own_pair)

    def split_rows(compute, *arrays):
        half = arrays[0].shape[0] // 2
        return [compute(*(array[at:to] for array in arrays)) for at, to in ((half, 2 * half), (0, half))]

    def dot_rows(first_mat, second_mat, second_dim):
        return lax.dot_general(
            first_mat,
            second_mat,
            (((first_mat.ndim - 1,), (second_dim,)), ((), ())),
            preferred_element_type=F32,
        )

    def local(
        tokens,
        lengths,
        norm_gain,
        mixer_in,
        lower_bound,
        head_gain,
        head_merge,
        feed_gain,
        gate_up,
        down_weight,
        out_grad,
    ):
        seqs, rows, model = tokens.shape
        dp_at = lax.axis_index("dp")
        z_at = lax.axis_index("tensor")
        half_at = z_at // 2
        role = 2 * (z_at % 2) + dp_at % 2

        def weight_grad(first_mat, second_mat):
            return lax.dot_general(
                first_mat.reshape(-1, first_mat.shape[-1]),
                second_mat.reshape(-1, second_mat.shape[-1]),
                (((0,), (0,)), ((), ())),
                preferred_element_type=F32,
            ).astype(BF)

        swap = half_at == 1
        lens = move(lengths, spreads[0])
        mixer_pair = spread_weight(mixer_in.reshape(mixer_in.shape[0], -1))
        vectors = [norm_gain, feed_gain, head_gain, lower_bound]
        vector_ends = np.cumsum([vector.shape[0] for vector in vectors])
        packed = jnp.zeros((dp_size, vector_ends[-1]), BF)
        packed = lax.dynamic_update_slice_in_dim(packed, jnp.concatenate(vectors)[None], dp_at, 0)
        packed = sum_steps(packed, high_steps)
        mixer_pair = [after(part, packed) for part in mixer_pair]
        tok = move(after(tokens, *mixer_pair), spreads[0])
        merge_pair = spread_weight(after(head_merge, tok))

        bounds = jnp.zeros((tensor_size, dp_size, lower_bound.shape[0]), BF)
        bounds = lax.dynamic_update_slice_in_dim(bounds, packed[None, :, vector_ends[2] :], z_at, 0)
        bounds = sum_steps(bounds, low_steps)
        vector_rows = packed.astype(F32)
        norm_vec = vector_rows[:, : vector_ends[0]].reshape(-1)
        feed_vec = vector_rows[:, vector_ends[0] : vector_ends[1]].reshape(-1)
        head_vec = vector_rows[:, vector_ends[1] : vector_ends[2]].reshape(1, -1)
        bound_vec = lax.dynamic_index_in_dim(bounds, role, 0, False).astype(F32).reshape(1, -1)

        positions = role * rows + jnp.arange(rows, dtype=jnp.int32)
        valid = (positions[None, :] < lens[:, None]).astype(F32)[:, :, None]
        own = role.astype(jnp.int32).reshape(1)

        masked = tok.astype(F32) * valid
        normed, scale_one = rms_rows(masked, norm_vec)
        normed = normed.astype(BF)
        gates_pair = spread_weight(after(gate_up.reshape(gate_up.shape[0], -1), normed, *merge_pair))
        down_pair = spread_weight(after(down_weight, *gates_pair))
        out_rows = move(after(out_grad, *down_pair), spreads[0])
        mixer_mat = gather_weight(joined(mixer_pair, swap))
        merge_mat = gather_weight(joined(merge_pair, swap))
        first_in = gather_rows(normed)
        gates_mat = gather_weight(joined([after(part, first_in) for part in gates_pair], swap))
        down_mat = gather_weight(joined(down_pair, swap))
        projected = dot_rows(first_in, mixer_mat, 0)
        mixed, head_out, states = recur_forward(own, projected, bound_vec, head_vec)
        attn = scatter_rows(*split_rows(lambda part: dot_rows(part, merge_mat, 0).astype(BF), head_out))
        middle = masked + attn
        normed_two, scale_two = rms_rows(middle, feed_vec)
        upstream = out_rows.astype(F32) * valid
        branch_in = gather_rows(upstream.astype(BF))
        second_in = after(gather_rows(normed_two.astype(BF)), branch_in)
        gate_pre = dot_rows(second_in, gates_mat, 0)
        hidden_cols = down_mat.shape[0]
        gate_part = gate_pre[..., :hidden_cols]
        up_part = gate_pre[..., hidden_cols:]
        sig_gate = jax.nn.sigmoid(gate_part)
        hidden = (gate_part * sig_gate * up_part).astype(BF)
        down_whole = weight_grad(hidden, branch_in)
        down_pair = scatter_grad(after(down_whole, down_mat))
        down_grad = return_grad(down_pair, swap)
        hidden_grad = dot_rows(after(branch_in, down_whole), down_mat, 1)
        gate_grad = hidden_grad * up_part * sig_gate * (1.0 + gate_part * (1.0 - sig_gate))
        up_grad = hidden_grad * gate_part * sig_gate
        both_grad = jnp.concatenate([gate_grad, up_grad], axis=-1).astype(BF)
        second_parts = split_rows(lambda part: dot_rows(part, gates_mat, 1).astype(BF), both_grad)
        second_far = scatter_far(second_parts[0])
        gates_whole = weight_grad(second_in, after(both_grad, second_far, *second_parts))
        second_far = move(second_far, z_swap)
        gates_pair = scatter_grad(after(gates_whole, down_pair, second_far))
        second_grad = after(scatter_own(second_far, second_parts[1]), gates_whole)
        middle_grad, feed_terms = norm_back(middle, scale_two, feed_vec, second_grad)
        middle_grad = middle_grad + upstream
        feed_parts = split_rows(lambda part: dot_rows(part, down_mat, 0).astype(BF), hidden)
        attn_in = after(gather_rows(middle_grad.astype(BF)), *feed_parts)
        feed_far = move(after(scatter_far(feed_parts[0]), attn_in), z_swap)
        feed_out = scatter_own(feed_far, feed_parts[1])
        block_out = move(after((valid * (middle + feed_out)).astype(BF), *down_grad), returns[0])
        out_head = dot_rows(attn_in, merge_mat, 1)
        proj_grad, bound_sum, head_sum = recur_backward(
            own, projected, mixed, out_head, states, bound_vec, head_vec
        )
        first_parts = split_rows(lambda part: dot_rows(part, mixer_mat, 1).astype(BF), proj_grad)
        first_far = move(scatter_far(first_parts[0]), z_swap)
        first_grad = scatter_own(first_far, first_parts[1])
        merge_whole = weight_grad(head_out, attn_in)
        mixer_whole = weight_grad(first_in, proj_grad)
        mixer_pair = scatter_grad(after(mixer_whole, gates_pair, *first_parts, *down_grad, block_out))
        gates_grad = return_grad(gates_pair, swap, block_out)
        first_grad = after(first_grad, merge_whole, mixer_whole, gates_grad[0])
        masked_grad, norm_terms = norm_back(masked, scale_one, norm_vec, first_grad)
        input_rows = (valid * (masked_grad + middle_grad)).astype(BF)

        merge_pair = scatter_grad(after(merge_whole, mixer_pair))
        input_grad = move(after(input_rows, *gates_grad), returns[0])
        mixer_grad = return_grad(mixer_pair, swap, input_grad)
        merge_grad = return_grad(merge_pair, swap, *mixer_grad)

        bound_all = jnp.zeros((tensor_size, bound_sum.shape[1]), F32)
        bound_all = lax.dynamic_update_slice_in_dim(bound_all, bound_sum, role, 0)
        sums = [
            jnp.sum(norm_terms, axis=(0, 1)),
            jnp.sum(feed_terms, axis=(0, 1)),
            head_sum.reshape(-1),
            bound_all.reshape(-1),
        ]
        ends = np.cumsum([part.shape[0] for part in sums])
        summed = sum_steps(jnp.concatenate(sums), [*high_steps, *low_steps])

        def shard_of(vector, count, at):
            return lax.dynamic_slice_in_dim(vector, at * count, count, 0)

        return (
            block_out,
            input_grad,
            shard_of(summed[: ends[0]], norm_gain.shape[0], dp_at),
            whole_grad(mixer_grad).reshape(mixer_in.shape),
            shard_of(summed[ends[2] :], lower_bound.shape[0], z_at * dp_size + dp_at),
            shard_of(summed[ends[1] : ends[2]], head_gain.shape[0], dp_at),
            whole_grad(merge_grad),
            shard_of(summed[ends[0] : ends[1]], feed_gain.shape[0], dp_at),
            whole_grad(gates_grad).reshape(gate_up.shape),
            whole_grad(down_grad),
        )

    return local


def solution(mesh):
    rows_spec = P("dp", "tensor", None)
    wide_spec = P("dp", None, "tensor")
    tall_spec = P(("tensor", "dp"), None)
    return jax.shard_map(
        make_local(mesh.shape["dp"], mesh.shape["tensor"]),
        mesh=mesh,
        in_specs=(
            rows_spec,
            P("dp"),
            P("dp"),
            wide_spec,
            P(("tensor", "dp")),
            P("dp"),
            tall_spec,
            P("dp"),
            wide_spec,
            tall_spec,
            rows_spec,
        ),
        out_specs=(
            rows_spec,
            rows_spec,
            P("dp"),
            wide_spec,
            P(("tensor", "dp")),
            P("dp"),
            tall_spec,
            P("dp"),
            wide_spec,
            tall_spec,
        ),
        check_vma=False,
    )
```
